128 devices in a mesh: rep: 16 (over y_lo, x, core), tp: 8 (over y_hi, z).
Axes of the slice: x: 4, y: 4 (y_hi: 2, y_lo: 2; y = y_hi * 2 + y_lo), z: 4, core: 2. Of those that a mesh axis runs over, the one named last changes fastest.
Arguments:
- pseudo_grads: float32 [16, 5120, 2048], P('rep', None, 'tp'), may hold values from -0.4375 to 0.4375
- outer_params: float32 [5120, 2048], P('rep', 'tp'), may hold values from -0.078125 to 0.078125
- momentum: float32 [5120, 2048], P('rep', 'tp'), may hold values from -0.21875 to 0.21875
- hidden_in: bfloat16 [4, 256, 5120], P(None, 'rep'), may hold values from -6 to 6
- queries: bfloat16 [4, 256, 5120], P(None, 'rep', 'tp')
- cache: bfloat16 [2, 256, 1024, 1024], P(None, 'rep', None, 'tp')
- lengths: int32 [256], P('rep'), may hold values from 2 to 1024, as said below
- out_weight: bfloat16 [5120, 5120], P('tp'), may hold values from -0.125 to 0.125
Outputs:
- new_params: float32 [5120, 2048], P('rep', 'tp')
- new_momentum: float32 [5120, 2048], P('rep', 'tp')
- new_kv: bfloat16 [4, 256, 2048], P(None, 'rep', 'tp')
- layer_out: bfloat16 [4, 256, 5120], P(None, 'rep', 'tp')
The draws below stay inside these ranges and needn't reach their ends.
Inputs may be any that keep to these rules, and one draw needn't show every extreme that they name: `lengths`: every row has at least 2 filled slots; in each aligned block of 16 rows some row has all 1024 slots filled.
All inputs are finite; a program needn't handle non-finite values.
Results may differ from the reference program's by a relative error of at most 0.0073.
Values may be sent and summed in bfloat16 or wider, within the bound.
A program may use at most 64 MiB of HBM per device.

```python
import jax
import jax.numpy as jnp
from jax import lax

D = 5120
QH = 40
KV = 8
HD = 128
ROW_DEV = 16
CACHE = 1024
STEPS = 4
ROWS = 256
KVW = 2048
QW = 5120
N_REP = 16


def first_keys(key):
    return jax.random.normal(key, (ROWS, KV * HD), jnp.float32)


def draw_cache(key, part):
    leading = first_keys(key)
    key = jax.random.fold_in(key, 11)
    values = jax.random.normal(key, (2, ROWS, CACHE, KV * HD), jnp.float32)
    values = values.at[0, :, 0, :].set(leading)
    return values.astype(jnp.bfloat16)


def draw_queries(key, part):
    key = jax.random.fold_in(key, 13)
    values = jax.random.normal(key, (STEPS, ROWS, QH * HD), jnp.float32)
    return values.astype(jnp.bfloat16)


def draw_lengths(key, part):
    key = jax.random.fold_in(key, 7)
    keys_split = jax.random.split(key, 5)
    drawn = jax.random.randint(keys_split[0], (ROWS,), 2, CACHE + 1)
    second = jax.random.randint(keys_split[1], (ROWS,), 2, CACHE + 1)
    third = jax.random.randint(keys_split[2], (ROWS,), 2, CACHE + 1)
    short_rows = jnp.minimum(jnp.minimum(drawn, second), third)
    coin = jax.random.randint(keys_split[3], (ROWS,), 0, 4) == 0
    result = jnp.where(coin, short_rows, second)
    groups = ROWS // ROW_DEV
    pick = jax.random.randint(keys_split[4], (groups, 1), 0, ROW_DEV)
    full_row = (jnp.arange(ROW_DEV)[None, :] == pick).reshape(ROWS)
    return jnp.where(full_row, CACHE, result).astype(jnp.int32)


def raised(entries, key, source, target, blocks, factor):
    owner, partner = [(jnp.arange(entries.shape[dim]) // (entries.shape[dim] // blocks)).reshape([-1 if axis == dim else 1 for axis in range(entries.ndim)]) for dim in (source, target)]
    chosen = jax.random.permutation(key, blocks)[partner]
    strong = (owner == chosen) | (owner == (partner + blocks // 2) % blocks)
    return jnp.where(strong, factor * entries, entries)


def block_scale(key, extent, shards, least, high):
    level = 1.0
    for dim, shards_of in shards:
        draws = jax.random.uniform(jax.random.fold_in(jax.random.fold_in(key, 6), dim), (shards_of,), jnp.float32, least / len(shards), high / len(shards))
        level = level * jnp.repeat(jnp.exp(draws), extent[dim] // shards_of).reshape((-1,) + (1,) * (len(extent) - 1 - dim))
    return level


def noise(key, dims, scale, reach, cuts=(), kind=jnp.bfloat16):
    factor_of = block_scale(key, dims, cuts, -0.22, 0.18) if cuts else 1.0
    drawn = jax.random.normal(key, dims, jnp.float32) * scale * factor_of
    return jnp.minimum(jnp.maximum(drawn, -reach), reach).astype(kind)


def bell_draw_with(stream_key, shape, spread, limit, pieces, heavy, kind=jnp.bfloat16):
    values = spread * jax.random.normal(stream_key, shape, jnp.float32)
    if pieces:
        values = values * block_scale(stream_key, shape, pieces, -0.22, 0.18)
    return jnp.clip(raised(values, jax.random.fold_in(stream_key, 3), *heavy), -limit, limit).astype(kind)


def setup_inputs(seed: int = 0) -> dict:
    streams_of = jax.random.split(jax.random.key(seed), 9)
    return {
        "pseudo_grads": bell_draw_with(streams_of[0], (N_REP, D, KVW), 0.02, 0.4375, ((0, 16), (2, 8)), (0, 1, 16, 2.0), jnp.float32),
        "outer_params": noise(streams_of[1], (D, KVW), D ** -0.5, 0.078125, ((0, 16), (1, 8)), jnp.float32),
        "momentum": noise(streams_of[2], (D, KVW), 0.014, 0.21875, ((0, 16), (1, 8)), jnp.float32),
        "hidden_in": noise(streams_of[3], (STEPS, ROWS, D), 1.0, 6.0, ((1, 16),)),
        "queries": draw_queries(jax.random.fold_in(streams_of[8], 71), 0),
        "cache": draw_cache(jax.random.fold_in(streams_of[8], 71), 0),
        "lengths": draw_lengths(jax.random.fold_in(streams_of[8], 71), 0),
        "out_weight": bell_draw_with(streams_of[7], (QW, D), QW ** -0.5, 0.125, ((0, 8),), (0, 1, 8, 2.0)),
    }


OUTER_RATE = 0.7
OUTER_DECAY = 0.9
ROPE_BASE = 1000000.0


def rotary(key_rows, positions):
    half_size = key_rows.shape[-1] // 2
    frequency = ROPE_BASE ** (-jnp.arange(half_size, dtype=jnp.float32) * 2.0 / key_rows.shape[-1])
    angles = positions.astype(jnp.float32)[..., None] * frequency
    cosine = jnp.cos(angles)
    sine = jnp.sin(angles)
    first_half = key_rows[..., :half_size]
    second_half = key_rows[..., half_size:]
    return jnp.concatenate([first_half * cosine - second_half * sine, second_half * cosine + first_half * sine], -1)


def reference(pseudo_grads, outer_params, momentum, hidden_in, queries, cache, lengths, out_weight):
    mean_grad = jnp.sum(pseudo_grads, axis=0) / N_REP
    new_momentum = OUTER_DECAY * momentum + mean_grad
    new_params = outer_params - OUTER_RATE * (mean_grad + OUTER_DECAY * new_momentum)
    weights = new_params.astype(jnp.bfloat16)
    flat_rows = hidden_in.reshape(STEPS * ROWS, D)
    fresh = jnp.dot(flat_rows, weights, preferred_element_type=jnp.float32).reshape(STEPS, ROWS, KV, 2, HD)
    positions = lengths[None, :] + jnp.arange(STEPS, dtype=jnp.int32)[:, None]
    new_keys = rotary(fresh[:, :, :, 0, :], positions[:, :, None]).astype(jnp.bfloat16)
    new_values = fresh[:, :, :, 1, :].astype(jnp.bfloat16)
    new_kv = jnp.stack([new_keys, new_values], 3).reshape(STEPS, ROWS, KVW)
    group_size = QH // KV
    score_scale = HD ** -0.5

    def one_row(inputs):
        query_row, key_cache, value_cache, key_new, value_new, row_length = inputs
        grouped = query_row.astype(jnp.float32).reshape(STEPS, KV, group_size, HD)
        cached_keys = key_cache.astype(jnp.float32).reshape(CACHE, KV, HD)
        cached_values = value_cache.astype(jnp.float32).reshape(CACHE, KV, HD)
        cache_scores = jnp.einsum('sgqd,jgd->sgqj', grouped, cached_keys) * score_scale
        filled = jnp.arange(CACHE, dtype=jnp.int32) < row_length
        cache_scores = jnp.where(filled[None, None, None, :], cache_scores, -1e30)
        fresh_scores = jnp.einsum('sgqd,ugd->sgqu', grouped, key_new.astype(jnp.float32)) * score_scale
        causal = jnp.arange(STEPS)[None, :] <= jnp.arange(STEPS)[:, None]
        fresh_scores = jnp.where(causal[:, None, None, :], fresh_scores, -1e30)
        peak_score = jnp.maximum(jnp.max(cache_scores, -1), jnp.max(fresh_scores, -1))[..., None]
        cache_exp = jnp.exp(cache_scores - peak_score)
        fresh_exp = jnp.exp(fresh_scores - peak_score)
        row_total = jnp.sum(cache_exp, -1, keepdims=True) + jnp.sum(fresh_exp, -1, keepdims=True)
        cache_probs = (cache_exp / row_total).astype(jnp.bfloat16)
        fresh_probs = (fresh_exp / row_total).astype(jnp.bfloat16)
        mixed = jnp.einsum('sgqj,jgd->sgqd', cache_probs.astype(jnp.float32), cached_values)
        mixed = mixed + jnp.einsum('sgqu,ugd->sgqd', fresh_probs.astype(jnp.float32), value_new.astype(jnp.float32))
        return mixed.astype(jnp.bfloat16).reshape(STEPS, QW)

    attention = lax.map(one_row, (jnp.transpose(queries, (1, 0, 2)), cache[0], cache[1],
                                  jnp.transpose(new_keys, (1, 0, 2, 3)), jnp.transpose(new_values, (1, 0, 2, 3)), lengths))
    attention = jnp.transpose(attention, (1, 0, 2)).reshape(STEPS * ROWS, QW)
    layer_out = jnp.dot(attention, out_weight, preferred_element_type=jnp.float32).astype(jnp.bfloat16).reshape(STEPS, ROWS, D)
    return new_params, new_momentum, new_kv, layer_out
```

```python
import functools

import jax
import jax.numpy as jnp
from jax import lax
from jax.experimental import pallas as pl
from jax.experimental.pallas import tpu as pltpu
from jax.sharding import PartitionSpec as P

HD = 128
GROUP = 5
REPLICAS = 16
STEPS = 4
OUTER_RATE = 0.7
OUTER_DECAY = 0.9
ROPE_BASE = 1000000.0
MASKED = -1e30
MESH = pl.DeviceIdType.MESH
BF16 = jnp.bfloat16
F32 = jnp.float32
OFFSETS = [(0, 0), (1, 2), (0, 2), (1, 1), (1, 3), (0, 1), (0, 3), (1, 0)]


def shifted(hi, lo, offset, sign=1):
    dy, dl = offset
    return lax.rem(hi + dy, 2), lax.rem(lo + (sign * dl) % 4, 4)


def kernel(
    g_hbm, par_hbm, mom_hbm, hid_hbm, q_hbm, cache_hbm, len_hbm, wo_hbm,
    newp_hbm, newm_hbm, kv_hbm, lo_hbm,
    g32, s0, r0, p1, r1, par, mom, wbuf, hsend, hbuf, fsend, frecv,
    qraw, qf, qb, kbuf, vbuf, lens, wo, acc, peak, total, cos_t, sin_t,
    kvb, osend, orecv, lob, newp, newm,
    g_sem, k_sem, v_sem, in_sem, out_sem,
    s0_send, s0_recv, p1_send, p1_recv, h1_send, h1_recv, h2_send, h2_recv,
    w_send, w_recv, f_send, f_recv, o_send, o_recv,
):
    rep = lax.axis_index("rep")
    tp = lax.axis_index("tp")
    core = lax.rem(rep, 2)
    chip = rep // 2
    yl, x = chip // 4, lax.rem(chip, 4)
    yh, z = tp // 4, lax.rem(tp, 4)
    rows_own = g32.shape[1]
    n_rows = qraw.shape[0]
    batch = n_rows // STEPS

    def chip_at(offset, sign=1):
        hi, lo = shifted(yl, x, offset, sign)
        return hi * 4 + lo

    def tp_at(offset, sign=1):
        hi, lo = shifted(yh, z, offset, sign)
        return hi * 4 + lo

    sibling = (rep + 1 - 2 * core, tp)

    def plane_dev(offset, sign=1):
        return (chip_at(offset, sign) * 2 + core, tp)

    g_copies = []
    for own in (0, 1):
        for k in range(8):
            block = chip_at(OFFSETS[k]) * 2 + (core if own else 1 - core)
            c = pltpu.make_async_copy(g_hbm.at[block], g32.at[own * 8 + k], g_sem.at[own * 8 + k])
            c.start()
            g_copies.append(c)
    width = hsend.shape[2]
    h_copies = []
    for k in range(8):
        col = pl.multiple_of(chip_at(OFFSETS[k]) * width, 128)
        src = hid_hbm.at[z, :, pl.ds(col, width)]
        dst = hsend.at[k] if k else hbuf.at[0, z]
        c = pltpu.make_async_copy(src, dst, in_sem.at[k])
        c.start()
        h_copies.append(c)

    barrier = pltpu.get_barrier_semaphore()
    pl.semaphore_signal(barrier, inc=1, device_id=sibling, device_id_type=MESH)
    for k in range(1, 8):
        pl.semaphore_signal(barrier, inc=1, device_id=plane_dev(OFFSETS[k]), device_id_type=MESH)
        pl.semaphore_signal(barrier, inc=1, device_id=(rep, tp_at(OFFSETS[k])), device_id_type=MESH)
    pl.semaphore_wait(barrier, 15)

    s0_copies = []
    for k in list(range(1, 8)) + [0]:
        g_copies[k].wait()
        s0[k] = g32[k].astype(BF16)
        c = pltpu.make_async_remote_copy(
            src_ref=s0.at[k], dst_ref=r0.at[k], send_sem=s0_send.at[k], recv_sem=s0_recv.at[k],
            device_id=sibling, device_id_type=MESH)
        c.start()
        s0_copies.append((k, c))
    h1_copies = []
    for k in range(8):
        h_copies[k].wait()
        if k:
            c = pltpu.make_async_remote_copy(
                src_ref=hsend.at[k], dst_ref=hbuf.at[k, z], send_sem=h1_send.at[k], recv_sem=h1_recv.at[k],
                device_id=plane_dev(OFFSETS[k]), device_id_type=MESH)
            c.start()
            h1_copies.append(c)

    small = [
        pltpu.make_async_copy(q_hbm, qraw, in_sem.at[8]),
        pltpu.make_async_copy(len_hbm, lens, in_sem.at[9]),
        pltpu.make_async_copy(par_hbm, par, in_sem.at[10]),
        pltpu.make_async_copy(mom_hbm, mom, in_sem.at[11]),
    ]
    for c in small:
        c.start()
    kv_copies = []
    for r in range(batch):
        ck = pltpu.make_async_copy(cache_hbm.at[0, r], kbuf.at[r], k_sem.at[r])
        cv = pltpu.make_async_copy(cache_hbm.at[1, r], vbuf.at[r], v_sem.at[r])
        ck.start()
        cv.start()
        kv_copies.append((ck, cv))
    wo_copy = pltpu.make_async_copy(wo_hbm, wo, in_sem.at[12])
    wo_copy.start()

    p1_copies = []
    for k, c in s0_copies:
        c.wait_recv()
        g_copies[8 + k].wait()
        if k:
            p1[k] = (g32[8 + k] + r0[k].astype(F32)).astype(BF16)
            c1 = pltpu.make_async_remote_copy(
                src_ref=p1.at[k], dst_ref=r1.at[k], send_sem=p1_send.at[k], recv_sem=p1_recv.at[k],
                device_id=plane_dev(OFFSETS[k]), device_id_type=MESH)
            c1.start()
            p1_copies.append(c1)

    for c in h1_copies:
        c.wait_recv()
    h2_copies = []
    for m in range(1, 4):
        c = pltpu.make_async_remote_copy(
            src_ref=hbuf.at[:, z], dst_ref=hbuf.at[:, z], send_sem=h2_send.at[m], recv_sem=h2_recv.at[m],
            device_id=(rep, tp_at((0, m))), device_id_type=MESH)
        c.start()
        h2_copies.append(c)

    for c in small:
        c.wait()
    for g in range(GROUP):
        part = qraw[:, g * HD:(g + 1) * HD]
        qb[g * n_rows:(g + 1) * n_rows, :] = part
        qf[g * n_rows:(g + 1) * n_rows, :] = part.astype(F32)
    qf[GROUP * n_rows:, :] = jnp.zeros((qf.shape[0] - GROUP * n_rows, HD), F32)
    row = lax.broadcasted_iota(jnp.int32, (n_rows, HD), 0)
    lane = lax.broadcasted_iota(jnp.int32, (n_rows, HD), 1)
    position = row // batch
    for r in range(batch):
        position = position + jnp.where(lax.rem(row, batch) == r, lens[r], 0)
    power = lax.rem(lane, HD // 2).astype(F32) * (-2.0 / HD)
    angle = position.astype(F32) * jnp.exp(power * jnp.log(jnp.float32(ROPE_BASE)))
    cos_t[...] = jnp.cos(angle)
    sine = jnp.sin(angle)
    sin_t[...] = jnp.where(lane < HD // 2, -sine, sine)

    scale = HD ** -0.5
    n_slots = kbuf.shape[1]
    per_row = qf.shape[0] // batch
    unroll = 4

    for r in range(batch):
        for c in kv_copies[r]:
            c.wait()

    def rows_body(i, carry):
        results = []
        for j in range(unroll):
            r = i * unroll + j
            q = qf[pl.ds(r, per_row, stride=batch), :].astype(BF16)
            scores = lax.dot_general(
                q, kbuf[r], (((1,), (1,)), ((), ())), preferred_element_type=F32) * scale
            slot = lax.broadcasted_iota(jnp.int32, scores.shape, 1)
            scores = jnp.where(slot < lens[r], scores, MASKED)
            top = jnp.max(scores, axis=1, keepdims=True)
            weight = jnp.exp(scores - top)
            mass = jnp.sum(weight, axis=1, keepdims=True)
            mixed = jnp.dot(weight.astype(BF16), vbuf[r], preferred_element_type=F32)
            results.append((r, top, mass, mixed))
        for r, top, mass, mixed in results:
            at = pl.ds(r, per_row, stride=batch)
            acc[at, :] = mixed
            peak[at, :] = jnp.broadcast_to(top, mixed.shape)
            total[at, :] = jnp.broadcast_to(mass, mixed.shape)
        return carry

    lax.fori_loop(0, batch // unroll, rows_body, 0)

    for c in p1_copies:
        c.wait_recv()
    grad = g32[8] + r0[0].astype(F32)
    for k in range(1, 8):
        grad = grad + r1[k].astype(F32)
    grad = grad * (1.0 / REPLICAS)
    moved = OUTER_DECAY * mom[...] + grad
    stepped = par[...] - OUTER_RATE * (grad + OUTER_DECAY * moved)
    newm[...] = moved
    newp[...] = stepped
    wbuf[core] = stepped.astype(BF16)
    w_copy = pltpu.make_async_remote_copy(
        src_ref=wbuf.at[core], dst_ref=wbuf.at[core], send_sem=w_send.at[0], recv_sem=w_recv.at[0],
        device_id=sibling, device_id_type=MESH)
    w_copy.start()
    out_copies = [
        pltpu.make_async_copy(newm, newm_hbm, out_sem.at[0]),
        pltpu.make_async_copy(newp, newp_hbm, out_sem.at[1]),
    ]
    for c in out_copies:
        c.start()

    for c in h2_copies:
        c.wait_recv()
    w_copy.wait_recv()
    weights = wbuf[...].reshape(2 * rows_own, wbuf.shape[2])
    f_copies = []
    fresh = None
    for k in [1, 2, 3, 4, 5, 6, 7, 0]:
        states = hbuf[k].reshape(n_rows, width)
        part = jnp.dot(states, weights, preferred_element_type=F32)
        if k:
            fsend[k] = part.astype(BF16)
            c = pltpu.make_async_remote_copy(
                src_ref=fsend.at[k], dst_ref=frecv.at[k], send_sem=f_send.at[k], recv_sem=f_recv.at[k],
                device_id=plane_dev(OFFSETS[k], -1), device_id_type=MESH)
            c.start()
            f_copies.append(c)
        else:
            fresh = part
    for k, c in zip(range(1, 8), f_copies):
        c.wait_recv()
        fresh = fresh + frecv[k].astype(F32)
    key_part = fresh[:, :HD]
    turned = pltpu.roll(key_part, HD // 2, 1)
    new_keys = (key_part * cos_t[...] + turned * sin_t[...]).astype(BF16)
    new_values = fresh[:, HD:].astype(BF16)
    kvb[:, :HD] = new_keys
    kvb[:, HD:] = new_values
    kv_out = pltpu.make_async_copy(kvb, kv_hbm, out_sem.at[2])
    kv_out.start()

    n_q = GROUP * n_rows
    scores = lax.dot_general(
        qb[...], new_keys, (((1,), (1,)), ((), ())), preferred_element_type=F32) * scale
    q_row = lax.broadcasted_iota(jnp.int32, scores.shape, 0)
    k_row = lax.broadcasted_iota(jnp.int32, scores.shape, 1)
    q_at = lax.rem(q_row, n_rows)
    allowed = (lax.rem(q_at, batch) == lax.rem(k_row, batch)) & (k_row <= q_at)
    scores = jnp.where(allowed, scores, MASKED)
    old_top = peak[:n_q, :1]
    top = jnp.maximum(old_top, jnp.max(scores, axis=1, keepdims=True))
    weight = jnp.exp(scores - top)
    shrink = jnp.exp(old_top - top)
    mass = total[:n_q, :1] * shrink + jnp.sum(weight, axis=1, keepdims=True)
    mixed = acc[:n_q, :] * shrink + jnp.dot(weight.astype(BF16), new_values, preferred_element_type=F32)
    mixed = (mixed / mass).astype(BF16)
    attention = jnp.concatenate([mixed[g * n_rows:(g + 1) * n_rows] for g in range(GROUP)], axis=1)

    wo_copy.wait()
    o_copies = []
    owned = None
    out_width = lob.shape[1]
    for k in [1, 2, 3, 4, 5, 6, 7, 0]:
        col = pl.multiple_of(tp_at(OFFSETS[k]) * out_width, 128)
        part = jnp.dot(attention, wo[:, pl.ds(col, out_width)], preferred_element_type=F32)
        if k:
            osend[k] = part.astype(BF16)
            c = pltpu.make_async_remote_copy(
                src_ref=osend.at[k], dst_ref=orecv.at[k], send_sem=o_send.at[k], recv_sem=o_recv.at[k],
                device_id=(rep, tp_at(OFFSETS[k])), device_id_type=MESH)
            c.start()
            o_copies.append(c)
        else:
            owned = part
    for k, c in zip(range(1, 8), o_copies):
        c.wait_recv()
        owned = owned + orecv[k].astype(F32)
    lob[...] = owned.astype(BF16)
    lo_out = pltpu.make_async_copy(lob, lo_hbm, out_sem.at[3])
    lo_out.start()

    for _, c in s0_copies:
        c.wait_send()
    for c in h1_copies + p1_copies + h2_copies + [w_copy] + f_copies + o_copies:
        c.wait_send()
    for c in out_copies + [kv_out, lo_out]:
        c.wait()


def per_device(
    pseudo_grads, outer_params, momentum, hidden_in, queries, cache, lengths, out_weight
):
    own, columns = outer_params.shape
    steps, batch, model = hidden_in.shape
    n_rows = steps * batch
    slots = cache.shape[2]
    features, out_all = out_weight.shape
    width = 2 * own
    out_width = out_all // 8
    g = pseudo_grads.reshape(REPLICAS, own, columns)
    dma = pltpu.SemaphoreType.DMA
    vm = pltpu.VMEM
    per_row = 24
    scratch = [
        vm((16, own, columns), F32),
        vm((8, own, columns), BF16),
        vm((8, own, columns), BF16),
        vm((8, own, columns), BF16),
        vm((8, own, columns), BF16),
        vm((own, columns), F32),
        vm((own, columns), F32),
        vm((2, own, columns), BF16),
        vm((8, batch, width), BF16),
        vm((8, steps, batch, width), BF16),
        vm((8, n_rows, columns), BF16),
        vm((8, n_rows, columns), BF16),
        vm((n_rows, features), BF16),
        vm((per_row * batch, HD), F32),
        vm((GROUP * n_rows, HD), BF16),
        vm((batch, slots, HD), BF16),
        vm((batch, slots, HD), BF16),
        pltpu.SMEM((batch,), jnp.int32),
        vm((features, out_all), BF16),
        vm((per_row * batch, HD), F32),
        vm((per_row * batch, HD), F32),
        vm((per_row * batch, HD), F32),
        vm((n_rows, HD), F32),
        vm((n_rows, HD), F32),
        vm((n_rows, columns), BF16),
        vm((8, n_rows, out_width), BF16),
        vm((8, n_rows, out_width), BF16),
        vm((n_rows, out_width), BF16),
        vm((own, columns), F32),
        vm((own, columns), F32),
        dma((16,)), dma((batch,)), dma((batch,)), dma((13,)), dma((4,)),
    ]
    for n in (8, 8, 8, 4, 1, 8, 8):
        scratch += [dma((n,)), dma((n,))]
    any_spec = pl.BlockSpec(memory_space=pl.ANY)
    new_params, new_momentum, new_kv, layer_out = pl.pallas_call(
        kernel,
        out_shape=(
            jax.ShapeDtypeStruct((own, columns), F32),
            jax.ShapeDtypeStruct((own, columns), F32),
            jax.ShapeDtypeStruct((n_rows, columns), BF16),
            jax.ShapeDtypeStruct((n_rows, out_width), BF16),
        ),
        in_specs=[any_spec] * 8,
        out_specs=(any_spec,) * 4,
        scratch_shapes=scratch,
        compiler_params=pltpu.CompilerParams(
            collective_id=0, has_side_effects=True, vmem_limit_bytes=52 * 1024 * 1024),
        name="outer_step_decode",
    )(
        g, outer_params, momentum, hidden_in, queries.reshape(n_rows, features),
        cache, lengths, out_weight,
    )
    return (
        new_params, new_momentum,
        new_kv.reshape(steps, batch, columns),
        layer_out.reshape(steps, batch, out_width),
    )


def solution(mesh):
    placed = (
        P("rep", None, "tp"),
        P("rep", "tp"),
        P("rep", "tp"),
        P(None, "rep", None),
        P(None, "rep", "tp"),
        P(None, "rep", None, "tp"),
        P("rep"),
        P("tp", None),
    )
    return jax.shard_map(
        per_device,
        mesh=mesh,
        in_specs=placed,
        out_specs=(P("rep", "tp"), P("rep", "tp"), P(None, "rep", "tp"), P(None, "rep", "tp")),
        check_vma=False,
    )
```

```python
import functools

import jax
import jax.numpy as jnp
from jax import lax
from jax.experimental import pallas as pl
from jax.experimental.pallas import tpu as pltpu
from jax.sharding import PartitionSpec as P

HD = 128
GROUP = 5
REPLICAS = 16
STEPS = 4
OUTER_RATE = 0.7
OUTER_DECAY = 0.9
ROPE_BASE = 1000000.0
MASKED = -1e30
MESH = pl.DeviceIdType.MESH
BF16 = jnp.bfloat16
F32 = jnp.float32
OFFSETS = [(1, 2), (0, 2), (1, 1), (0, 1), (1, 3), (0, 3), (1, 0), (0, 0)]
TP_OFFSETS = [(1, 2), (0, 2), (1, 1), (1, 3), (0, 1), (0, 3), (1, 0), (0, 0)]


def shifted(hi, lo, offset, sign=1):
    dy, dl = offset
    return lax.rem(hi + dy, 2), lax.rem(lo + (sign * dl) % 4, 4)


def kernel(
    g_hbm, par_hbm, mom_hbm, hid_hbm, q_hbm, cache_hbm, len_hbm, wo_hbm,
    newp, newm, kvb, lob,
    g32, s0, r0, c1s, c1r, c2s, c2r, d1s, d1r, d2s, d2r,
    par, mom, wbuf, hsend, hbuf, fsend, frecv,
    qraw, qf, qb, kbuf, vbuf, lens, wo, acc, peak, total, cos_t, sin_t, osend, orecv,
    g_sem, k_sem, v_sem, in_sem,
    s0_send, s0_recv, c1_send, c1_recv, c2_send, c2_recv, d1_send, d1_recv, d2_send, d2_recv,
    h1_send, h1_recv, h2_send, h2_recv, w_send, w_recv, f_send, f_recv, o_send, o_recv,
):
    rep = lax.axis_index("rep")
    tp = lax.axis_index("tp")
    core = lax.rem(rep, 2)
    chip = rep // 2
    yl, x = chip // 4, lax.rem(chip, 4)
    yh, z = tp // 4, lax.rem(tp, 4)
    rows_own = g32.shape[1]
    n_rows = qraw.shape[0]
    batch = n_rows // STEPS

    def chip_at(offset, sign=1):
        hi, lo = shifted(yl, x, offset, sign)
        return hi * 4 + lo

    def tp_at(offset, sign=1):
        hi, lo = shifted(yh, z, offset, sign)
        return hi * 4 + lo

    sibling = (rep + 1 - 2 * core, tp)

    def plane_dev(offset, sign=1):
        return (chip_at(offset, sign) * 2 + core, tp)

    g_copies = []
    for own in (0, 1):
        for k in range(8):
            block = chip_at(OFFSETS[k]) * 2 + (core if own else 1 - core)
            c = pltpu.make_async_copy(g_hbm.at[block], g32.at[own * 8 + k], g_sem.at[own * 8 + k])
            c.start()
            g_copies.append(c)
    width = hsend.shape[2]
    h_copies = []
    for k in range(8):
        col = pl.multiple_of(chip_at(OFFSETS[k]) * width, 128)
        src = hid_hbm.at[z, :, pl.ds(col, width)]
        dst = hsend.at[k] if k < 7 else hbuf.at[7, z]
        c = pltpu.make_async_copy(src, dst, in_sem.at[k])
        c.start()
        h_copies.append(c)

    barrier = pltpu.get_barrier_semaphore()
    pl.semaphore_signal(barrier, inc=1, device_id=sibling, device_id_type=MESH)
    for k in range(7):
        pl.semaphore_signal(barrier, inc=1, device_id=plane_dev(OFFSETS[k]), device_id_type=MESH)
        pl.semaphore_signal(barrier, inc=1, device_id=(rep, tp_at(TP_OFFSETS[k])), device_id_type=MESH)
    sent = []

    def send(src, dst, send_sem, recv_sem, device):
        c = pltpu.make_async_remote_copy(
            src_ref=src, dst_ref=dst, send_sem=send_sem, recv_sem=recv_sem,
            device_id=device, device_id_type=MESH)
        c.start()
        sent.append(c)
        return c

    s0_copies = []
    for k in range(8):
        g_copies[k].wait()
        s0[k] = g32[k].astype(BF16)
        if k == 3:
            pl.semaphore_wait(barrier, 15)
        if k >= 3:
            for m in range(4 if k == 3 else 1):
                n = m if k == 3 else k
                s0_copies.append(send(s0.at[n], r0.at[n], s0_send.at[n], s0_recv.at[n], sibling))
    h1_copies = []
    for k in range(8):
        h_copies[k].wait()
        if k < 7:
            h1_copies.append(send(
                hsend.at[k], hbuf.at[k, z], h1_send.at[k], h1_recv.at[k], plane_dev(OFFSETS[k])))

    small = [
        pltpu.make_async_copy(q_hbm, qraw, in_sem.at[8]),
        pltpu.make_async_copy(len_hbm, lens, in_sem.at[9]),
        pltpu.make_async_copy(par_hbm, par, in_sem.at[10]),
        pltpu.make_async_copy(mom_hbm, mom, in_sem.at[11]),
    ]
    for c in small:
        c.start()
    kv_copies = []
    for r in range(batch):
        ck = pltpu.make_async_copy(cache_hbm.at[0, r], kbuf.at[r], k_sem.at[r])
        cv = pltpu.make_async_copy(cache_hbm.at[1, r], vbuf.at[r], v_sem.at[r])
        ck.start()
        cv.start()
        kv_copies.append((ck, cv))
    wo_copy = pltpu.make_async_copy(wo_hbm, wo, in_sem.at[12])
    wo_copy.start()

    upper = c1s.shape[1]
    c1_copies, d1_copies = {}, {}
    for k, (dy, dx) in enumerate(OFFSETS):
        s0_copies[k].wait_recv()
        g_copies[8 + k].wait()
        both = g32[8 + k] + r0[k].astype(F32)
        if dy:
            c1s[dx] = both[:upper].astype(BF16)
            c1_copies[dx] = send(
                c1s.at[dx], c1r.at[dx], c1_send.at[dx], c1_recv.at[dx], plane_dev((1, 0)))
        else:
            g32[8 + k, :upper, :] = both[:upper]
        if dx:
            d1s[dx, dy] = both[upper:].astype(BF16)
            if not dy:
                d1_copies[dx] = send(
                    d1s.at[dx], d1r.at[dx], d1_send.at[dx], d1_recv.at[dx], plane_dev((0, dx)))
        else:
            g32[8 + k, upper:, :] = both[upper:]
    slot_of = {offset: 8 + k for k, offset in enumerate(OFFSETS)}

    for c in h1_copies:
        c.wait_recv()
    h2_copies = []
    for m in range(1, 4):
        h2_copies.append(send(
            hbuf.at[:, z], hbuf.at[:, z], h2_send.at[m], h2_recv.at[m], (rep, tp_at((0, m)))))

    for c in small:
        c.wait()
    for g in range(GROUP):
        part = qraw[:, g * HD:(g + 1) * HD]
        qb[g * n_rows:(g + 1) * n_rows, :] = part
        qf[g * n_rows:(g + 1) * n_rows, :] = part.astype(F32)
    qf[GROUP * n_rows:, :] = jnp.zeros((qf.shape[0] - GROUP * n_rows, HD), F32)

    scale = HD ** -0.5
    per_row = qf.shape[0] // batch

    def attend(rows):
        results = []
        for r in rows:
            for c in kv_copies[r]:
                c.wait()
        for r in rows:
            q = qf[pl.ds(r, per_row, stride=batch), :].astype(BF16)
            scores = lax.dot_general(
                q, kbuf[r], (((1,), (1,)), ((), ())), preferred_element_type=F32) * scale
            slot = lax.broadcasted_iota(jnp.int32, scores.shape, 1)
            scores = jnp.where(slot < lens[r], scores, MASKED)
            top = jnp.max(scores, axis=1, keepdims=True)
            weight = jnp.exp(scores - top)
            mass = jnp.sum(weight, axis=1, keepdims=True)
            mixed = jnp.dot(weight.astype(BF16), vbuf[r], preferred_element_type=F32)
            results.append((r, top, mass, mixed))
        for r, top, mass, mixed in results:
            at = pl.ds(r, per_row, stride=batch)
            acc[at, :] = mixed
            peak[at, :] = jnp.broadcast_to(top, mixed.shape)
            total[at, :] = jnp.broadcast_to(mass, mixed.shape)

    attend(range(0, 2))
    c2_copies = []
    for n, dx in enumerate((2, 1, 3)):
        c1_copies[dx].wait_recv()
        c2s[dx] = (g32[slot_of[0, dx], :upper, :] + c1r[dx].astype(F32)).astype(BF16)
        c2_copies.append(send(c2s.at[dx], c2r.at[dx], c2_send.at[dx], c2_recv.at[dx], plane_dev((0, dx))))
        attend(range(2 + 2 * n, 4 + 2 * n))
    lower_sum = g32[slot_of[1, 0], upper:, :]
    for dx in (2, 1, 3):
        d1_copies[dx].wait_recv()
        lower_sum = lower_sum + d1r[dx, 1].astype(F32)
    d2s[...] = lower_sum.astype(BF16)
    d2_copy = send(d2s, d2r, d2_send.at[0], d2_recv.at[0], plane_dev((1, 0)))
    attend(range(8, 12))
    row = lax.broadcasted_iota(jnp.int32, (n_rows, HD), 0)
    lane = lax.broadcasted_iota(jnp.int32, (n_rows, HD), 1)
    position = row // batch
    for r in range(batch):
        position = position + jnp.where(lax.rem(row, batch) == r, lens[r], 0)
    power = lax.rem(lane, HD // 2).astype(F32) * (-2.0 / HD)
    angle = position.astype(F32) * jnp.exp(power * jnp.log(jnp.float32(ROPE_BASE)))
    cos_t[...] = jnp.cos(angle)
    sine = jnp.sin(angle)
    sin_t[...] = jnp.where(lane < HD // 2, -sine, sine)

    def outer_step(rows, summed):
        grad = summed * (1.0 / REPLICAS)
        moved = OUTER_DECAY * mom[rows, :] + grad
        stepped = par[rows, :] - OUTER_RATE * (grad + OUTER_DECAY * moved)
        newm[rows, :] = moved
        newp[rows, :] = stepped
        wbuf[core, rows, :] = stepped.astype(BF16)

    mine = slot_of[0, 0]
    c1_copies[0].wait_recv()
    upper_sum = g32[mine, :upper, :] + c1r[0].astype(F32)
    for n, dx in enumerate((2, 1, 3)):
        c2_copies[n].wait_recv()
        upper_sum = upper_sum + c2r[dx].astype(F32)
    outer_step(slice(0, upper), upper_sum)
    w_copies = [send(
        wbuf.at[core, pl.ds(0, upper)], wbuf.at[core, pl.ds(0, upper)], w_send.at[0], w_recv.at[0], sibling)]
    d2_copy.wait_recv()
    lower_sum = g32[mine, upper:, :] + d2r[...].astype(F32)
    for dx in (1, 2, 3):
        lower_sum = lower_sum + d1r[dx, 0].astype(F32)
    outer_step(slice(upper, rows_own), lower_sum)
    lower = rows_own - upper
    w_copies.append(send(
        wbuf.at[core, pl.ds(upper, lower)], wbuf.at[core, pl.ds(upper, lower)], w_send.at[1], w_recv.at[1],
        sibling))
    attend(range(12, 14))

    for c in h2_copies:
        c.wait_recv()
    for c in w_copies:
        c.wait_recv()
    weights = wbuf[...].reshape(2 * rows_own, wbuf.shape[2])
    f_copies = []
    fresh = None
    for k in range(8):
        states = hbuf[k].reshape(n_rows, width)
        part = jnp.dot(states, weights, preferred_element_type=F32)
        if k < 7:
            fsend[k] = part.astype(BF16)
            f_copies.append(send(
                fsend.at[k], frecv.at[k], f_send.at[k], f_recv.at[k], plane_dev(OFFSETS[k], -1)))
        else:
            fresh = part
    attend(range(14, 16))
    for k, c in enumerate(f_copies):
        c.wait_recv()
        fresh = fresh + frecv[k].astype(F32)
    key_part = fresh[:, :HD]
    turned = pltpu.roll(key_part, HD // 2, 1)
    new_keys = (key_part * cos_t[...] + turned * sin_t[...]).astype(BF16)
    new_values = fresh[:, HD:].astype(BF16)
    kvb[:, :HD] = new_keys
    kvb[:, HD:] = new_values

    n_q = GROUP * n_rows
    scores = lax.dot_general(
        qb[...], new_keys, (((1,), (1,)), ((), ())), preferred_element_type=F32) * scale
    q_row = lax.broadcasted_iota(jnp.int32, scores.shape, 0)
    k_row = lax.broadcasted_iota(jnp.int32, scores.shape, 1)
    q_at = lax.rem(q_row, n_rows)
    allowed = (lax.rem(q_at, batch) == lax.rem(k_row, batch)) & (k_row <= q_at)
    scores = jnp.where(allowed, scores, MASKED)
    old_top = peak[:n_q, :1]
    top = jnp.maximum(old_top, jnp.max(scores, axis=1, keepdims=True))
    weight = jnp.exp(scores - top)
    shrink = jnp.exp(old_top - top)
    mass = total[:n_q, :1] * shrink + jnp.sum(weight, axis=1, keepdims=True)
    mixed = acc[:n_q, :] * shrink + jnp.dot(weight.astype(BF16), new_values, preferred_element_type=F32)
    mixed = (mixed / mass).astype(BF16)
    attention = jnp.concatenate([mixed[g * n_rows:(g + 1) * n_rows] for g in range(GROUP)], axis=1)

    wo_copy.wait()
    o_copies = []
    owned = None
    out_width = lob.shape[1]
    for k in range(8):
        col = pl.multiple_of(tp_at(TP_OFFSETS[k]) * out_width, 128)
        part = jnp.dot(attention, wo[:, pl.ds(col, out_width)], preferred_element_type=F32)
        if k < 7:
            osend[k] = part.astype(BF16)
            o_copies.append(send(
                osend.at[k], orecv.at[k], o_send.at[k], o_recv.at[k], (rep, tp_at(TP_OFFSETS[k]))))
        else:
            owned = part
    for k, c in enumerate(o_copies):
        c.wait_recv()
        owned = owned + orecv[k].astype(F32)
    lob[...] = owned.astype(BF16)
    for c in sent:
        c.wait_send()


def finish(*refs):
    ins, outs, sem = refs[:4], refs[4:8], refs[8]
    copies = [pltpu.make_async_copy(a, b, sem.at[i]) for i, (a, b) in enumerate(zip(ins, outs))]
    for c in copies:
        c.start()
    for c in copies:
        c.wait()


def per_device(
    pseudo_grads, outer_params, momentum, hidden_in, queries, cache, lengths, out_weight
):
    own, columns = outer_params.shape
    steps, batch, model = hidden_in.shape
    n_rows = steps * batch
    slots = cache.shape[2]
    features, out_all = out_weight.shape
    width = 2 * own
    out_width = out_all // 8
    g = pseudo_grads.reshape(REPLICAS, own, columns)
    dma = pltpu.SemaphoreType.DMA
    vm = pltpu.VMEM
    per_row = 24
    upper = 192
    scratch = [
        vm((16, own, columns), F32),
        vm((8, own, columns), BF16),
        vm((8, own, columns), BF16),
        vm((4, upper, columns), BF16),
        vm((4, upper, columns), BF16),
        vm((4, upper, columns), BF16),
        vm((4, upper, columns), BF16),
        vm((4, 2, own - upper, columns), BF16),
        vm((4, 2, own - upper, columns), BF16),
        vm((own - upper, columns), BF16),
        vm((own - upper, columns), BF16),
        vm((own, columns), F32),
        vm((own, columns), F32),
        vm((2, own, columns), BF16),
        vm((8, batch, width), BF16),
        vm((8, steps, batch, width), BF16),
        vm((8, n_rows, columns), BF16),
        vm((8, n_rows, columns), BF16),
        vm((n_rows, features), BF16),
        vm((per_row * batch, HD), F32),
        vm((GROUP * n_rows, HD), BF16),
        vm((batch, slots, HD), BF16),
        vm((batch, slots, HD), BF16),
        pltpu.SMEM((batch,), jnp.int32),
        vm((features, out_all), BF16),
        vm((per_row * batch, HD), F32),
        vm((per_row * batch, HD), F32),
        vm((per_row * batch, HD), F32),
        vm((n_rows, HD), F32),
        vm((n_rows, HD), F32),
        vm((8, n_rows, out_width), BF16),
        vm((8, n_rows, out_width), BF16),
        dma((16,)), dma((batch,)), dma((batch,)), dma((13,)),
    ]
    for n in (8, 4, 4, 4, 1, 8, 4, 2, 8, 8):
        scratch += [dma((n,)), dma((n,))]
    any_spec = pl.BlockSpec(memory_space=pl.ANY)
    new_params, new_momentum, new_kv, layer_out = pl.pallas_call(
        kernel,
        out_shape=(
            pltpu.VMEM((own, columns), F32),
            pltpu.VMEM((own, columns), F32),
            pltpu.VMEM((n_rows, columns), BF16),
            pltpu.VMEM((n_rows, out_width), BF16),
        ),
        in_specs=[any_spec] * 8,
        out_specs=(pl.BlockSpec(memory_space=pltpu.VMEM),) * 4,
        scratch_shapes=scratch,
        compiler_params=pltpu.CompilerParams(
            collective_id=0, has_side_effects=True, vmem_limit_bytes=56 * 1024 * 1024),
        name="outer_step_decode",
    )(
        *(pltpu.with_memory_space_constraint(a, pltpu.HBM) for a in (
            g, outer_params, momentum, hidden_in, queries.reshape(n_rows, features),
            cache, lengths, out_weight)),
    )
    new_params, new_momentum, new_kv, layer_out = pl.pallas_call(
        finish,
        out_shape=tuple(jax.ShapeDtypeStruct(a.shape, a.dtype) for a in (new_params, new_momentum, new_kv, layer_out)),
        in_specs=[any_spec] * 4,
        out_specs=(any_spec,) * 4,
        scratch_shapes=[dma((4,))],
        name="finish",
    )(*(pltpu.with_memory_space_constraint(a, pltpu.VMEM) for a in (new_params, new_momentum, new_kv, layer_out)))
    return (
        new_params, new_momentum,
        new_kv.reshape(steps, batch, columns),
        layer_out.reshape(steps, batch, out_width),
    )


def solution(mesh):
    placed = (
        P("rep", None, "tp"),
        P("rep", "tp"),
        P("rep", "tp"),
        P(None, "rep", None),
        P(None, "rep", "tp"),
        P(None, "rep", None, "tp"),
        P("rep"),
        P("tp", None),
    )
    return jax.shard_map(
        per_device,
        mesh=mesh,
        in_specs=placed,
        out_specs=(P("rep", "tp"), P("rep", "tp"), P(None, "rep", "tp"), P(None, "rep", "tp")),
        check_vma=False,
    )
```

```python
import functools

import jax
import jax.numpy as jnp
from jax import lax
from jax.experimental import pallas as pl
from jax.experimental.pallas import tpu as pltpu
from jax.sharding import PartitionSpec as P

HD = 128
GROUP = 5
REPLICAS = 16
STEPS = 4
OUTER_RATE = 0.7
OUTER_DECAY = 0.9
ROPE_BASE = 1000000.0
MASKED = -1e30
MESH = pl.DeviceIdType.MESH
BF16 = jnp.bfloat16
F32 = jnp.float32
OFFSETS = [(1, 2), (0, 2), (1, 1), (0, 1), (1, 3), (0, 3), (1, 0), (0, 0)]
TP_OFFSETS = [(1, 2), (0, 2), (1, 1), (1, 3), (0, 1), (0, 3), (1, 0), (0, 0)]


def shifted(hi, lo, offset, sign=1):
    dy, dl = offset
    return lax.rem(hi + dy, 2), lax.rem(lo + (sign * dl) % 4, 4)


def kernel(
    g_hbm, par_hbm, mom_hbm, hid_hbm, q_hbm, cache_hbm, len_hbm, wo_hbm,
    newp, newm, kvb, lob,
    g32, s0, r0, c1s, c1r, c2s, c2r, d1s, d1r, d2s, d2r,
    par, mom, wbuf, hsend, hbuf, fsend, frecv,
    qraw, qf, qb, kbuf, vbuf, lens, wo, acc, peak, total, cos_t, sin_t, osend, orecv,
    g_sem, k_sem, v_sem, in_sem,
    s0_send, s0_recv, c1_send, c1_recv, c2_send, c2_recv, d1_send, d1_recv, d2_send, d2_recv,
    h1_send, h1_recv, h2_send, h2_recv, w_send, w_recv, f_send, f_recv, o_send, o_recv,
):
    rep = lax.axis_index("rep")
    tp = lax.axis_index("tp")
    core = lax.rem(rep, 2)
    chip = rep // 2
    yl, x = chip // 4, lax.rem(chip, 4)
    yh, z = tp // 4, lax.rem(tp, 4)
    rows_own = g32.shape[1]
    n_rows = qraw.shape[0]
    batch = n_rows // STEPS
    half = n_rows // 2

    def chip_at(offset, sign=1):
        hi, lo = shifted(yl, x, offset, sign)
        return hi * 4 + lo

    def tp_at(offset, sign=1):
        hi, lo = shifted(yh, z, offset, sign)
        return hi * 4 + lo

    sibling = (rep + 1 - 2 * core, tp)

    def plane_dev(offset, sign=1):
        return (chip_at(offset, sign) * 2 + core, tp)

    def across(dx):
        return (((1 - yl) * 4 + lax.rem(x + dx, 4)) * 2 + core, (1 - yh) * 4 + z)

    g_copies = []
    for own in (0, 1):
        for k in range(8):
            block = chip_at(OFFSETS[k]) * 2 + (core if own else 1 - core)
            c = pltpu.make_async_copy(g_hbm.at[block], g32.at[own * 8 + k], g_sem.at[own * 8 + k])
            c.start()
            g_copies.append(c)
    width = hsend.shape[2]
    h_copies = []
    for k in range(8):
        col = pl.multiple_of(chip_at(OFFSETS[k]) * width, 128)
        src = hid_hbm.at[z, :, pl.ds(col, width)]
        dst = hsend.at[k] if k < 7 else hbuf.at[7, z]
        c = pltpu.make_async_copy(src, dst, in_sem.at[k])
        c.start()
        h_copies.append(c)

    barrier = pltpu.get_barrier_semaphore()
    pl.semaphore_signal(barrier, inc=1, device_id=sibling, device_id_type=MESH)
    for dx in range(4):
        pl.semaphore_signal(barrier, inc=1, device_id=across(dx), device_id_type=MESH)
    for k in range(7):
        pl.semaphore_signal(barrier, inc=1, device_id=plane_dev(OFFSETS[k]), device_id_type=MESH)
        pl.semaphore_signal(barrier, inc=1, device_id=(rep, tp_at(TP_OFFSETS[k])), device_id_type=MESH)
    sent = []

    def send(src, dst, send_sem, recv_sem, device):
        c = pltpu.make_async_remote_copy(
            src_ref=src, dst_ref=dst, send_sem=send_sem, recv_sem=recv_sem,
            device_id=device, device_id_type=MESH)
        c.start()
        sent.append(c)
        return c

    s0_copies = []
    for k in range(8):
        g_copies[k].wait()
        s0[k] = g32[k].astype(BF16)
        if k == 3:
            pl.semaphore_wait(barrier, 19)
        if k >= 3:
            for m in range(4 if k == 3 else 1):
                n = m if k == 3 else k
                s0_copies.append(send(s0.at[n], r0.at[n], s0_send.at[n], s0_recv.at[n], sibling))
    h1_copies = []
    for k, (dy, dx) in enumerate(OFFSETS):
        h_copies[k].wait()
        if k < 7:
            h1_copies.append(send(
                hsend.at[k], hbuf.at[k, z], h1_send.at[k], h1_recv.at[k],
                across(dx) if dy else plane_dev((0, dx))))

    small = [
        pltpu.make_async_copy(q_hbm, qraw, in_sem.at[8]),
        pltpu.make_async_copy(len_hbm, lens, in_sem.at[9]),
        pltpu.make_async_copy(par_hbm, par, in_sem.at[10]),
        pltpu.make_async_copy(mom_hbm, mom, in_sem.at[11]),
    ]
    for c in small:
        c.start()
    kv_copies = []
    for r in range(batch):
        ck = pltpu.make_async_copy(cache_hbm.at[0, r], kbuf.at[r], k_sem.at[r])
        cv = pltpu.make_async_copy(cache_hbm.at[1, r], vbuf.at[r], v_sem.at[r])
        ck.start()
        cv.start()
        kv_copies.append((ck, cv))
    wo_copy = pltpu.make_async_copy(wo_hbm, wo, in_sem.at[12])
    wo_copy.start()

    upper = c1s.shape[1]
    c1_copies, d1_copies = {}, {}
    for k, (dy, dx) in enumerate(OFFSETS):
        s0_copies[k].wait_recv()
        g_copies[8 + k].wait()
        both = g32[8 + k] + r0[k].astype(F32)
        if dy:
            c1s[dx] = both[:upper].astype(BF16)
            c1_copies[dx] = send(
                c1s.at[dx], c1r.at[dx], c1_send.at[dx], c1_recv.at[dx], plane_dev((1, 0)))
        else:
            g32[8 + k, :upper, :] = both[:upper]
        if dx:
            d1s[dx, dy] = both[upper:].astype(BF16)
            if not dy:
                d1_copies[dx] = send(
                    d1s.at[dx], d1r.at[dx], d1_send.at[dx], d1_recv.at[dx], plane_dev((0, dx)))
        else:
            g32[8 + k, upper:, :] = both[upper:]
    slot_of = {offset: 8 + k for k, offset in enumerate(OFFSETS)}

    for c in h1_copies:
        c.wait_recv()
    h2_copies = []
    for m in range(1, 4):
        h2_copies.append(send(
            hbuf.at[:, z], hbuf.at[:, z], h2_send.at[m], h2_recv.at[m], (rep, tp_at((0, m)))))

    for c in small:
        c.wait()
    for g in range(GROUP):
        part = qraw[:, g * HD:(g + 1) * HD]
        for h in range(2):
            qb[h, g * half:(g + 1) * half, :] = part[h * half:(h + 1) * half]
        qf[g * n_rows:(g + 1) * n_rows, :] = part.astype(F32)
    qf[GROUP * n_rows:, :] = jnp.zeros((qf.shape[0] - GROUP * n_rows, HD), F32)

    scale = HD ** -0.5
    per_row = qf.shape[0] // batch

    def attend(rows):
        results = []
        for r in rows:
            for c in kv_copies[r]:
                c.wait()
        for r in rows:
            q = qf[pl.ds(r, per_row, stride=batch), :].astype(BF16)
            scores = lax.dot_general(
                q, kbuf[r], (((1,), (1,)), ((), ())), preferred_element_type=F32) * scale
            slot = lax.broadcasted_iota(jnp.int32, scores.shape, 1)
            scores = jnp.where(slot < lens[r], scores, MASKED)
            top = jnp.max(scores, axis=1, keepdims=True)
            weight = jnp.exp(scores - top)
            mass = jnp.sum(weight, axis=1, keepdims=True)
            mixed = jnp.dot(weight.astype(BF16), vbuf[r], preferred_element_type=F32)
            results.append((r, top, mass, mixed))
        for r, top, mass, mixed in results:
            at = pl.ds(r, per_row, stride=batch)
            acc[at, :] = mixed
            peak[at, :] = jnp.broadcast_to(top, mixed.shape)
            total[at, :] = jnp.broadcast_to(mass, mixed.shape)

    attend(range(0, 2))
    c2_copies = []
    for n, dx in enumerate((2, 1, 3)):
        c1_copies[dx].wait_recv()
        c2s[dx] = (g32[slot_of[0, dx], :upper, :] + c1r[dx].astype(F32)).astype(BF16)
        c2_copies.append(send(c2s.at[dx], c2r.at[dx], c2_send.at[dx], c2_recv.at[dx], plane_dev((0, dx))))
        attend(range(2 + 2 * n, 4 + 2 * n))
    lower_sum = g32[slot_of[1, 0], upper:, :]
    for dx in (2, 1, 3):
        d1_copies[dx].wait_recv()
        lower_sum = lower_sum + d1r[dx, 1].astype(F32)
    d2s[...] = lower_sum.astype(BF16)
    d2_copy = send(d2s, d2r, d2_send.at[0], d2_recv.at[0], plane_dev((1, 0)))
    attend(range(8, 12))
    row = lax.broadcasted_iota(jnp.int32, (n_rows, HD), 0)
    lane = lax.broadcasted_iota(jnp.int32, (n_rows, HD), 1)
    position = row // batch
    for r in range(batch):
        position = position + jnp.where(lax.rem(row, batch) == r, lens[r], 0)
    power = lax.rem(lane, HD // 2).astype(F32) * (-2.0 / HD)
    angle = position.astype(F32) * jnp.exp(power * jnp.log(jnp.float32(ROPE_BASE)))
    cos_t[...] = jnp.cos(angle)
    sine = jnp.sin(angle)
    sin_t[...] = jnp.where(lane < HD // 2, -sine, sine)

    def outer_step(rows, summed):
        grad = summed * (1.0 / REPLICAS)
        moved = OUTER_DECAY * mom[rows, :] + grad
        stepped = par[rows, :] - OUTER_RATE * (grad + OUTER_DECAY * moved)
        newm[rows, :] = moved
        newp[rows, :] = stepped
        wbuf[core, rows, :] = stepped.astype(BF16)

    mine = slot_of[0, 0]
    c1_copies[0].wait_recv()
    upper_sum = g32[mine, :upper, :] + c1r[0].astype(F32)
    for n, dx in enumerate((2, 1, 3)):
        c2_copies[n].wait_recv()
        upper_sum = upper_sum + c2r[dx].astype(F32)
    outer_step(slice(0, upper), upper_sum)
    w_copies = [send(
        wbuf.at[core, pl.ds(0, upper)], wbuf.at[core, pl.ds(0, upper)], w_send.at[0], w_recv.at[0], sibling)]
    d2_copy.wait_recv()
    lower_sum = g32[mine, upper:, :] + d2r[...].astype(F32)
    for dx in (1, 2, 3):
        lower_sum = lower_sum + d1r[dx, 0].astype(F32)
    outer_step(slice(upper, rows_own), lower_sum)
    lower = rows_own - upper
    w_copies.append(send(
        wbuf.at[core, pl.ds(upper, lower)], wbuf.at[core, pl.ds(upper, lower)], w_send.at[1], w_recv.at[1],
        sibling))
    attend(range(12, 14))

    for c in h2_copies:
        c.wait_recv()
    for c in w_copies:
        c.wait_recv()
    weights = wbuf[...].reshape(2 * rows_own, wbuf.shape[2])
    f_copies, fresh = [], []
    for h in range(2):
        states = hbuf[:, h * (STEPS // 2):(h + 1) * (STEPS // 2)].reshape(8 * half, width)
        part = jnp.dot(states, weights, preferred_element_type=F32)
        at = pl.ds(h * half, half)
        for k in range(7):
            fsend[k, at, :] = part[k * half:(k + 1) * half].astype(BF16)
            f_copies.append(send(
                fsend.at[k, at], frecv.at[k, at], f_send.at[7 * h + k], f_recv.at[7 * h + k],
                plane_dev(OFFSETS[k], -1)))
        fresh.append(part[7 * half:])
    attend(range(14, 16))

    o_copies, owned = [], []
    out_width = lob.shape[1]
    keys, values = [], []
    for h in range(2):
        at = pl.ds(h * half, half)
        now = fresh[h]
        for k in range(7):
            f_copies[7 * h + k].wait_recv()
            now = now + frecv[k, at, :].astype(F32)
        key_part = now[:, :HD]
        turned = pltpu.roll(key_part, HD // 2, 1)
        keys.append((key_part * cos_t[at, :] + turned * sin_t[at, :]).astype(BF16))
        values.append(now[:, HD:].astype(BF16))
        kvb[at, :HD] = keys[h]
        kvb[at, HD:] = values[h]

        def gather(ref):
            return jnp.concatenate(
                [ref[g * n_rows + h * half:g * n_rows + (h + 1) * half, :] for g in range(GROUP)], axis=0)

        scores = lax.dot_general(
            qb[h], jnp.concatenate(keys, axis=0), (((1,), (1,)), ((), ())), preferred_element_type=F32) * scale
        q_row = lax.broadcasted_iota(jnp.int32, scores.shape, 0)
        k_row = lax.broadcasted_iota(jnp.int32, scores.shape, 1)
        q_at = lax.rem(q_row, half) + h * half
        allowed = (lax.rem(q_at, batch) == lax.rem(k_row, batch)) & (k_row <= q_at)
        scores = jnp.where(allowed, scores, MASKED)
        old_top = gather(peak)[:, :1]
        top = jnp.maximum(old_top, jnp.max(scores, axis=1, keepdims=True))
        weight = jnp.exp(scores - top)
        shrink = jnp.exp(old_top - top)
        mass = gather(total)[:, :1] * shrink + jnp.sum(weight, axis=1, keepdims=True)
        mixed = gather(acc) * shrink + jnp.dot(
            weight.astype(BF16), jnp.concatenate(values, axis=0), preferred_element_type=F32)
        mixed = (mixed / mass).astype(BF16)
        attention = jnp.concatenate([mixed[g * half:(g + 1) * half] for g in range(GROUP)], axis=1)

        if h == 0:
            wo_copy.wait()
        for k in range(8):
            col = pl.multiple_of(tp_at(TP_OFFSETS[k]) * out_width, 128)
            part = jnp.dot(attention, wo[:, pl.ds(col, out_width)], preferred_element_type=F32)
            if k < 7:
                osend[k, at, :] = part.astype(BF16)
                o_copies.append(send(
                    osend.at[k, at], orecv.at[k, at], o_send.at[7 * h + k], o_recv.at[7 * h + k],
                    (rep, tp_at(TP_OFFSETS[k]))))
            else:
                owned.append(part)
    for h in range(2):
        at = pl.ds(h * half, half)
        now = owned[h]
        for k in range(7):
            o_copies[7 * h + k].wait_recv()
            now = now + orecv[k, at, :].astype(F32)
        lob[at, :] = now.astype(BF16)
    for c in sent:
        c.wait_send()


def finish(*refs):
    ins, outs, sem = refs[:4], refs[4:8], refs[8]
    copies = [pltpu.make_async_copy(a, b, sem.at[i]) for i, (a, b) in enumerate(zip(ins, outs))]
    for c in copies:
        c.start()
    for c in copies:
        c.wait()


def per_device(
    pseudo_grads, outer_params, momentum, hidden_in, queries, cache, lengths, out_weight
):
    own, columns = outer_params.shape
    steps, batch, model = hidden_in.shape
    n_rows = steps * batch
    slots = cache.shape[2]
    features, out_all = out_weight.shape
    width = 2 * own
    out_width = out_all // 8
    g = pseudo_grads.reshape(REPLICAS, own, columns)
    dma = pltpu.SemaphoreType.DMA
    vm = pltpu.VMEM
    per_row = 24
    upper = 192
    scratch = [
        vm((16, own, columns), F32),
        vm((8, own, columns), BF16),
        vm((8, own, columns), BF16),
        vm((4, upper, columns), BF16),
        vm((4, upper, columns), BF16),
        vm((4, upper, columns), BF16),
        vm((4, upper, columns), BF16),
        vm((4, 2, own - upper, columns), BF16),
        vm((4, 2, own - upper, columns), BF16),
        vm((own - upper, columns), BF16),
        vm((own - upper, columns), BF16),
        vm((own, columns), F32),
        vm((own, columns), F32),
        vm((2, own, columns), BF16),
        vm((8, batch, width), BF16),
        vm((8, steps, batch, width), BF16),
        vm((8, n_rows, columns), BF16),
        vm((8, n_rows, columns), BF16),
        vm((n_rows, features), BF16),
        vm((per_row * batch, HD), F32),
        vm((2, GROUP * n_rows // 2, HD), BF16),
        vm((batch, slots, HD), BF16),
        vm((batch, slots, HD), BF16),
        pltpu.SMEM((batch,), jnp.int32),
        vm((features, out_all), BF16),
        vm((per_row * batch, HD), F32),
        vm((per_row * batch, HD), F32),
        vm((per_row * batch, HD), F32),
        vm((n_rows, HD), F32),
        vm((n_rows, HD), F32),
        vm((8, n_rows, out_width), BF16),
        vm((8, n_rows, out_width), BF16),
        dma((16,)), dma((batch,)), dma((batch,)), dma((13,)),
    ]
    for n in (8, 4, 4, 4, 1, 8, 4, 2, 14, 14):
        scratch += [dma((n,)), dma((n,))]
    any_spec = pl.BlockSpec(memory_space=pl.ANY)
    new_params, new_momentum, new_kv, layer_out = pl.pallas_call(
        kernel,
        out_shape=(
            pltpu.VMEM((own, columns), F32),
            pltpu.VMEM((own, columns), F32),
            pltpu.VMEM((n_rows, columns), BF16),
            pltpu.VMEM((n_rows, out_width), BF16),
        ),
        in_specs=[any_spec] * 8,
        out_specs=(pl.BlockSpec(memory_space=pltpu.VMEM),) * 4,
        scratch_shapes=scratch,
        compiler_params=pltpu.CompilerParams(
            collective_id=0, has_side_effects=True, vmem_limit_bytes=56 * 1024 * 1024),
        name="outer_step_decode",
    )(
        *(pltpu.with_memory_space_constraint(a, pltpu.HBM) for a in (
            g, outer_params, momentum, hidden_in, queries.reshape(n_rows, features),
            cache, lengths, out_weight)),
    )
    new_params, new_momentum, new_kv, layer_out = pl.pallas_call(
        finish,
        out_shape=tuple(jax.ShapeDtypeStruct(a.shape, a.dtype) for a in (new_params, new_momentum, new_kv, layer_out)),
        in_specs=[any_spec] * 4,
        out_specs=(any_spec,) * 4,
        scratch_shapes=[dma((4,))],
        name="finish",
    )(*(pltpu.with_memory_space_constraint(a, pltpu.VMEM) for a in (new_params, new_momentum, new_kv, layer_out)))
    return (
        new_params, new_momentum,
        new_kv.reshape(steps, batch, columns),
        layer_out.reshape(steps, batch, out_width),
    )


def solution(mesh):
    placed = (
        P("rep", None, "tp"),
        P("rep", "tp"),
        P("rep", "tp"),
        P(None, "rep", None),
        P(None, "rep", "tp"),
        P(None, "rep", None, "tp"),
        P("rep"),
        P("tp", None),
    )
    return jax.shard_map(
        per_device,
        mesh=mesh,
        in_specs=placed,
        out_specs=(P("rep", "tp"), P("rep", "tp"), P(None, "rep", "tp"), P(None, "rep", "tp")),
        check_vma=False,
    )
```

```python
import functools

import jax
import jax.numpy as jnp
from jax import lax
from jax.experimental import pallas as pl
from jax.experimental.pallas import tpu as pltpu
from jax.sharding import PartitionSpec as P

HD = 128
GROUP = 5
REPLICAS = 16
STEPS = 4
OUTER_RATE = 0.7
OUTER_DECAY = 0.9
ROPE_BASE = 1000000.0
MASKED = -1e30
MESH = pl.DeviceIdType.MESH
BF16 = jnp.bfloat16
F32 = jnp.float32
OFFSETS = [(1, 2), (0, 2), (1, 1), (0, 1), (1, 3), (0, 3), (1, 0), (0, 0)]
TP_OFFSETS = [(1, 2), (0, 2), (1, 1), (1, 3), (0, 1), (0, 3), (1, 0), (0, 0)]


def shifted(hi, lo, offset, sign=1):
    dy, dl = offset
    return lax.rem(hi + dy, 2), lax.rem(lo + (sign * dl) % 4, 4)


def kernel(
    g_hbm, par_hbm, mom_hbm, hid_hbm, q_hbm, cache_hbm, len_hbm, wo_hbm,
    newp, newm, kvb, lob,
    g32, s0, r0, c1s, c1r, c2s, c2r, d1s, d1r, d2s, d2r,
    par, mom, wbuf, hsend, hbuf, fsend, frecv,
    qraw, qf, qb, kbuf, vbuf, lens, wo, acc, peak, total, cos_t, sin_t, osend, orecv,
    g_sem, k_sem, v_sem, in_sem,
    s0_send, s0_recv, c1_send, c1_recv, c2_send, c2_recv, d1_send, d1_recv, d2_send, d2_recv,
    h1_send, h1_recv, h2_send, h2_recv, w_send, w_recv, f_send, f_recv, o_send, o_recv,
):
    rep = lax.axis_index("rep")
    tp = lax.axis_index("tp")
    core = lax.rem(rep, 2)
    chip = rep // 2
    yl, x = chip // 4, lax.rem(chip, 4)
    yh, z = tp // 4, lax.rem(tp, 4)
    rows_own = g32.shape[1]
    n_rows = qraw.shape[0]
    batch = n_rows // STEPS
    half = n_rows // 2

    def chip_at(offset, sign=1):
        hi, lo = shifted(yl, x, offset, sign)
        return hi * 4 + lo

    def tp_at(offset, sign=1):
        hi, lo = shifted(yh, z, offset, sign)
        return hi * 4 + lo

    sibling = (rep + 1 - 2 * core, tp)

    def plane_dev(offset, sign=1):
        return (chip_at(offset, sign) * 2 + core, tp)

    def across(dx):
        return (((1 - yl) * 4 + lax.rem(x + dx, 4)) * 2 + core, (1 - yh) * 4 + z)

    width = hsend.shape[2]
    h_copies = []
    for k in range(8):
        col = pl.multiple_of(chip_at(OFFSETS[k]) * width, 128)
        src = hid_hbm.at[z, :, pl.ds(col, width)]
        dst = hsend.at[k] if k < 7 else hbuf.at[7, z]
        c = pltpu.make_async_copy(src, dst, in_sem.at[k])
        c.start()
        h_copies.append(c)

    g_copies = []
    for own in (0, 1):
        for k in range(8):
            block = chip_at(OFFSETS[k]) * 2 + (core if own else 1 - core)
            c = pltpu.make_async_copy(g_hbm.at[block], g32.at[own * 8 + k], g_sem.at[own * 8 + k])
            c.start()
            g_copies.append(c)
    barrier = pltpu.get_barrier_semaphore()
    pl.semaphore_signal(barrier, inc=1, device_id=sibling, device_id_type=MESH)
    for dx in range(4):
        pl.semaphore_signal(barrier, inc=1, device_id=across(dx), device_id_type=MESH)
    for k in range(7):
        pl.semaphore_signal(barrier, inc=1, device_id=plane_dev(OFFSETS[k]), device_id_type=MESH)
        pl.semaphore_signal(barrier, inc=1, device_id=(rep, tp_at(TP_OFFSETS[k])), device_id_type=MESH)
    sent = []

    def send(src, dst, send_sem, recv_sem, device):
        c = pltpu.make_async_remote_copy(
            src_ref=src, dst_ref=dst, send_sem=send_sem, recv_sem=recv_sem,
            device_id=device, device_id_type=MESH)
        c.start()
        sent.append(c)
        return c

    s0_copies = []

    def share(n):
        s0_copies.append(send(s0.at[n], r0.at[n], s0_send.at[n], s0_recv.at[n], sibling))

    early = 3
    for k in range(early):
        g_copies[k].wait()
        s0[k] = g32[k].astype(BF16)
    pl.semaphore_wait(barrier, 19)
    for k in range(early):
        share(k)

    h1_copies = []
    for k, (dy, dx) in enumerate(OFFSETS):
        h_copies[k].wait()
        if k < 7:
            h1_copies.append(send(
                hsend.at[k], hbuf.at[k, z], h1_send.at[k], h1_recv.at[k],
                across(dx) if dy else plane_dev((0, dx))))
    for k in range(early, 8):
        g_copies[k].wait()
        s0[k] = g32[k].astype(BF16)
        share(k)

    small = [
        pltpu.make_async_copy(q_hbm, qraw, in_sem.at[8]),
        pltpu.make_async_copy(len_hbm, lens, in_sem.at[9]),
        pltpu.make_async_copy(par_hbm, par, in_sem.at[10]),
        pltpu.make_async_copy(mom_hbm, mom, in_sem.at[11]),
    ]
    for c in small:
        c.start()
    kv_copies = []
    for r in range(batch):
        ck = pltpu.make_async_copy(cache_hbm.at[0, r], kbuf.at[r], k_sem.at[r])
        cv = pltpu.make_async_copy(cache_hbm.at[1, r], vbuf.at[r], v_sem.at[r])
        ck.start()
        cv.start()
        kv_copies.append((ck, cv))
    wo_copy = pltpu.make_async_copy(wo_hbm, wo, in_sem.at[12])
    wo_copy.start()

    upper = c1s.shape[1]
    c1_copies, d1_copies = {}, {}
    for k, (dy, dx) in enumerate(OFFSETS):
        s0_copies[k].wait_recv()
        g_copies[8 + k].wait()
        both = g32[8 + k] + r0[k].astype(F32)
        if dy:
            c1s[dx] = both[:upper].astype(BF16)
            c1_copies[dx] = send(
                c1s.at[dx], c1r.at[dx], c1_send.at[dx], c1_recv.at[dx], plane_dev((1, 0)))
        else:
            g32[8 + k, :upper, :] = both[:upper]
        if dx:
            d1s[dx, dy] = both[upper:].astype(BF16)
            if not dy:
                d1_copies[dx] = send(
                    d1s.at[dx], d1r.at[dx], d1_send.at[dx], d1_recv.at[dx], plane_dev((0, dx)))
        else:
            g32[8 + k, upper:, :] = both[upper:]
    slot_of = {offset: 8 + k for k, offset in enumerate(OFFSETS)}

    for c in small:
        c.wait()
    for g in range(GROUP):
        part = qraw[:, g * HD:(g + 1) * HD]
        for h in range(2):
            qb[h, g * half:(g + 1) * half, :] = part[h * half:(h + 1) * half]
        qf[g * n_rows:(g + 1) * n_rows, :] = part.astype(F32)
    qf[GROUP * n_rows:, :] = jnp.zeros((qf.shape[0] - GROUP * n_rows, HD), F32)

    scale = HD ** -0.5
    per_row = qf.shape[0] // batch

    def attend(rows):
        results = []
        for r in rows:
            for c in kv_copies[r]:
                c.wait()
        for r in rows:
            q = qf[pl.ds(r, per_row, stride=batch), :].astype(BF16)
            scores = lax.dot_general(
                q, kbuf[r], (((1,), (1,)), ((), ())), preferred_element_type=F32) * scale
            slot = lax.broadcasted_iota(jnp.int32, scores.shape, 1)
            scores = jnp.where(slot < lens[r], scores, MASKED)
            top = jnp.max(scores, axis=1, keepdims=True)
            weight = jnp.exp(scores - top)
            mass = jnp.sum(weight, axis=1, keepdims=True)
            mixed = jnp.dot(weight.astype(BF16), vbuf[r], preferred_element_type=F32)
            results.append((r, top, mass, mixed))
        for r, top, mass, mixed in results:
            at = pl.ds(r, per_row, stride=batch)
            acc[at, :] = mixed
            peak[at, :] = jnp.broadcast_to(top, mixed.shape)
            total[at, :] = jnp.broadcast_to(mass, mixed.shape)

    attend(range(0, 2))
    c2_copies = []
    for n, dx in enumerate((2, 1, 3)):
        c1_copies[dx].wait_recv()
        c2s[dx] = (g32[slot_of[0, dx], :upper, :] + c1r[dx].astype(F32)).astype(BF16)
        for dx in ((), (1, 2), (3,))[n]:
            c2_copies.append(send(c2s.at[dx], c2r.at[dx], c2_send.at[dx], c2_recv.at[dx], plane_dev((0, dx))))
        if n == 0:
            for c in h1_copies:
                c.wait_recv()
            h2_copies = []
            for m in range(1, 4):
                h2_copies.append(send(
                    hbuf.at[:, z], hbuf.at[:, z], h2_send.at[m], h2_recv.at[m], (rep, tp_at((0, m)))))
        attend(range(2 + 2 * n, 4 + 2 * n))
    lower_sum = g32[slot_of[1, 0], upper:, :]
    for dx in (2, 1, 3):
        d1_copies[dx].wait_recv()
        lower_sum = lower_sum + d1r[dx, 1].astype(F32)
    d2s[...] = lower_sum.astype(BF16)
    d2_copy = send(d2s, d2r, d2_send.at[0], d2_recv.at[0], plane_dev((1, 0)))
    attend(range(8, 12))
    row = lax.broadcasted_iota(jnp.int32, (n_rows, HD), 0)
    lane = lax.broadcasted_iota(jnp.int32, (n_rows, HD), 1)
    position = row // batch
    for r in range(batch):
        position = position + jnp.where(lax.rem(row, batch) == r, lens[r], 0)
    power = lax.rem(lane, HD // 2).astype(F32) * (-2.0 / HD)
    angle = position.astype(F32) * jnp.exp(power * jnp.log(jnp.float32(ROPE_BASE)))
    cos_t[...] = jnp.cos(angle)
    sine = jnp.sin(angle)
    sin_t[...] = jnp.where(lane < HD // 2, -sine, sine)

    def outer_step(rows, summed):
        grad = summed * (1.0 / REPLICAS)
        moved = OUTER_DECAY * mom[rows, :] + grad
        stepped = par[rows, :] - OUTER_RATE * (grad + OUTER_DECAY * moved)
        newm[rows, :] = moved
        newp[rows, :] = stepped
        wbuf[core, rows, :] = stepped.astype(BF16)

    mine = slot_of[0, 0]
    c1_copies[0].wait_recv()
    upper_sum = g32[mine, :upper, :] + c1r[0].astype(F32)
    for n, dx in enumerate((1, 2, 3)):
        c2_copies[n].wait_recv()
        upper_sum = upper_sum + c2r[dx].astype(F32)
    outer_step(slice(0, upper), upper_sum)
    w_copies = [send(
        wbuf.at[core, pl.ds(0, upper)], wbuf.at[core, pl.ds(0, upper)], w_send.at[0], w_recv.at[0], sibling)]
    d2_copy.wait_recv()
    lower_sum = g32[mine, upper:, :] + d2r[...].astype(F32)
    for dx in (1, 2, 3):
        lower_sum = lower_sum + d1r[dx, 0].astype(F32)
    outer_step(slice(upper, rows_own), lower_sum)
    lower = rows_own - upper
    w_copies.append(send(
        wbuf.at[core, pl.ds(upper, lower)], wbuf.at[core, pl.ds(upper, lower)], w_send.at[1], w_recv.at[1],
        sibling))
    attend(range(12, 14))

    for c in h2_copies:
        c.wait_recv()
    for c in w_copies:
        c.wait_recv()
    weights = wbuf[...].reshape(2 * rows_own, wbuf.shape[2])
    f_copies, fresh = [], []
    for h in range(2):
        states = hbuf[:, h * (STEPS // 2):(h + 1) * (STEPS // 2)].reshape(8 * half, width)
        part = jnp.dot(states, weights, preferred_element_type=F32)
        at = pl.ds(h * half, half)
        for k in range(7):
            fsend[k, at, :] = part[k * half:(k + 1) * half].astype(BF16)
            f_copies.append(send(
                fsend.at[k, at], frecv.at[k, at], f_send.at[7 * h + k], f_recv.at[7 * h + k],
                plane_dev(OFFSETS[k], -1)))
        fresh.append(part[7 * half:])
    attend(range(14, 16))

    o_copies, owned = [], []
    out_width = lob.shape[1]
    keys, values = [], []
    for h in range(2):
        at = pl.ds(h * half, half)
        now = fresh[h]
        for k in range(7):
            f_copies[7 * h + k].wait_recv()
            now = now + frecv[k, at, :].astype(F32)
        key_part = now[:, :HD]
        turned = pltpu.roll(key_part, HD // 2, 1)
        keys.append((key_part * cos_t[at, :] + turned * sin_t[at, :]).astype(BF16))
        values.append(now[:, HD:].astype(BF16))
        kvb[at, :HD] = keys[h]
        kvb[at, HD:] = values[h]

        def gather(ref):
            return jnp.concatenate(
                [ref[g * n_rows + h * half:g * n_rows + (h + 1) * half, :] for g in range(GROUP)], axis=0)

        scores = lax.dot_general(
            qb[h], jnp.concatenate(keys, axis=0), (((1,), (1,)), ((), ())), preferred_element_type=F32) * scale
        q_row = lax.broadcasted_iota(jnp.int32, scores.shape, 0)
        k_row = lax.broadcasted_iota(jnp.int32, scores.shape, 1)
        q_at = lax.rem(q_row, half) + h * half
        allowed = (lax.rem(q_at, batch) == lax.rem(k_row, batch)) & (k_row <= q_at)
        scores = jnp.where(allowed, scores, MASKED)
        old_top = gather(peak)[:, :1]
        top = jnp.maximum(old_top, jnp.max(scores, axis=1, keepdims=True))
        weight = jnp.exp(scores - top)
        shrink = jnp.exp(old_top - top)
        mass = gather(total)[:, :1] * shrink + jnp.sum(weight, axis=1, keepdims=True)
        mixed = gather(acc) * shrink + jnp.dot(
            weight.astype(BF16), jnp.concatenate(values, axis=0), preferred_element_type=F32)
        mixed = (mixed / mass).astype(BF16)
        attention = jnp.concatenate([mixed[g * half:(g + 1) * half] for g in range(GROUP)], axis=1)

        if h == 0:
            wo_copy.wait()
        for k in range(8):
            col = pl.multiple_of(tp_at(TP_OFFSETS[k]) * out_width, 128)
            part = jnp.dot(attention, wo[:, pl.ds(col, out_width)], preferred_element_type=F32)
            if k < 7:
                osend[k, at, :] = part.astype(BF16)
                o_copies.append(send(
                    osend.at[k, at], orecv.at[k, at], o_send.at[7 * h + k], o_recv.at[7 * h + k],
                    (rep, tp_at(TP_OFFSETS[k]))))
            else:
                owned.append(part)
    for h in range(2):
        at = pl.ds(h * half, half)
        now = owned[h]
        for k in range(7):
            o_copies[7 * h + k].wait_recv()
            now = now + orecv[k, at, :].astype(F32)
        lob[at, :] = now.astype(BF16)
    for c in sent:
        c.wait_send()


def finish(*refs):
    ins, outs, sem = refs[:4], refs[4:8], refs[8]
    copies = [pltpu.make_async_copy(a, b, sem.at[i]) for i, (a, b) in enumerate(zip(ins, outs))]
    for c in copies:
        c.start()
    for c in copies:
        c.wait()


def per_device(
    pseudo_grads, outer_params, momentum, hidden_in, queries, cache, lengths, out_weight
):
    own, columns = outer_params.shape
    steps, batch, model = hidden_in.shape
    n_rows = steps * batch
    slots = cache.shape[2]
    features, out_all = out_weight.shape
    width = 2 * own
    out_width = out_all // 8
    g = pseudo_grads.reshape(REPLICAS, own, columns)
    dma = pltpu.SemaphoreType.DMA
    vm = pltpu.VMEM
    per_row = 24
    upper = 192
    scratch = [
        vm((16, own, columns), F32),
        vm((8, own, columns), BF16),
        vm((8, own, columns), BF16),
        vm((4, upper, columns), BF16),
        vm((4, upper, columns), BF16),
        vm((4, upper, columns), BF16),
        vm((4, upper, columns), BF16),
        vm((4, 2, own - upper, columns), BF16),
        vm((4, 2, own - upper, columns), BF16),
        vm((own - upper, columns), BF16),
        vm((own - upper, columns), BF16),
        vm((own, columns), F32),
        vm((own, columns), F32),
        vm((2, own, columns), BF16),
        vm((8, batch, width), BF16),
        vm((8, steps, batch, width), BF16),
        vm((8, n_rows, columns), BF16),
        vm((8, n_rows, columns), BF16),
        vm((n_rows, features), BF16),
        vm((per_row * batch, HD), F32),
        vm((2, GROUP * n_rows // 2, HD), BF16),
        vm((batch, slots, HD), BF16),
        vm((batch, slots, HD), BF16),
        pltpu.SMEM((batch,), jnp.int32),
        vm((features, out_all), BF16),
        vm((per_row * batch, HD), F32),
        vm((per_row * batch, HD), F32),
        vm((per_row * batch, HD), F32),
        vm((n_rows, HD), F32),
        vm((n_rows, HD), F32),
        vm((8, n_rows, out_width), BF16),
        vm((8, n_rows, out_width), BF16),
        dma((16,)), dma((batch,)), dma((batch,)), dma((13,)),
    ]
    for n in (8, 4, 4, 4, 1, 8, 4, 2, 14, 14):
        scratch += [dma((n,)), dma((n,))]
    any_spec = pl.BlockSpec(memory_space=pl.ANY)
    new_params, new_momentum, new_kv, layer_out = pl.pallas_call(
        kernel,
        out_shape=(
            pltpu.VMEM((own, columns), F32),
            pltpu.VMEM((own, columns), F32),
            pltpu.VMEM((n_rows, columns), BF16),
            pltpu.VMEM((n_rows, out_width), BF16),
        ),
        in_specs=[any_spec] * 8,
        out_specs=(pl.BlockSpec(memory_space=pltpu.VMEM),) * 4,
        scratch_shapes=scratch,
        compiler_params=pltpu.CompilerParams(
            collective_id=0, has_side_effects=True, vmem_limit_bytes=56 * 1024 * 1024),
        name="outer_step_decode",
    )(
        *(pltpu.with_memory_space_constraint(a, pltpu.HBM) for a in (
            g, outer_params, momentum, hidden_in, queries.reshape(n_rows, features),
            cache, lengths, out_weight)),
    )
    new_params, new_momentum, new_kv, layer_out = pl.pallas_call(
        finish,
        out_shape=tuple(jax.ShapeDtypeStruct(a.shape, a.dtype) for a in (new_params, new_momentum, new_kv, layer_out)),
        in_specs=[any_spec] * 4,
        out_specs=(any_spec,) * 4,
        scratch_shapes=[dma((4,))],
        name="finish",
    )(*(pltpu.with_memory_space_constraint(a, pltpu.VMEM) for a in (new_params, new_momentum, new_kv, layer_out)))
    return (
        new_params, new_momentum,
        new_kv.reshape(steps, batch, columns),
        layer_out.reshape(steps, batch, out_width),
    )


def solution(mesh):
    placed = (
        P("rep", None, "tp"),
        P("rep", "tp"),
        P("rep", "tp"),
        P(None, "rep", None),
        P(None, "rep", "tp"),
        P(None, "rep", None, "tp"),
        P("rep"),
        P("tp", None),
    )
    return jax.shard_map(
        per_device,
        mesh=mesh,
        in_specs=placed,
        out_specs=(P("rep", "tp"), P("rep", "tp"), P(None, "rep", "tp"), P(None, "rep", "tp")),
        check_vma=False,
    )
```

```python
import functools

import jax
import jax.numpy as jnp
from jax import lax
from jax.experimental import pallas as pl
from jax.experimental.pallas import tpu as pltpu
from jax.sharding import PartitionSpec as P

HD = 128
GROUP = 5
REPLICAS = 16
STEPS = 4
OUTER_RATE = 0.7
OUTER_DECAY = 0.9
ROPE_BASE = 1000000.0
MASKED = -1e30
MESH = pl.DeviceIdType.MESH
BF16 = jnp.bfloat16
F32 = jnp.float32
OFFSETS = [(1, 2), (0, 2), (1, 1), (0, 1), (1, 3), (0, 3), (1, 0), (0, 0)]
TP_OFFSETS = [(1, 2), (0, 2), (1, 1), (1, 3), (0, 1), (0, 3), (1, 0), (0, 0)]


def shifted(hi, lo, offset, sign=1):
    dy, dl = offset
    return lax.rem(hi + dy, 2), lax.rem(lo + (sign * dl) % 4, 4)


def kernel(
    g_hbm, par_hbm, mom_hbm, hid_hbm, q_hbm, cache_hbm, len_hbm, wo_hbm,
    newp, newm, kvb, lob,
    g32, s0, r0, c1s, c1r, c2s, c2r, d1s, d1r, d2s, d2r,
    par, mom, wbuf, hsend, hbuf, fsend, frecv,
    qraw, qf, qb, kbuf, vbuf, lens, wo, acc, peak, total, cos_t, sin_t, osend, orecv,
    g_sem, k_sem, v_sem, in_sem,
    s0_send, s0_recv, c1_send, c1_recv, c2_send, c2_recv, d1_send, d1_recv, d2_send, d2_recv,
    h1_send, h1_recv, h2_send, h2_recv, w_send, w_recv, f_send, f_recv, o_send, o_recv,
):
    rep = lax.axis_index("rep")
    tp = lax.axis_index("tp")
    core = lax.rem(rep, 2)
    chip = rep // 2
    yl, x = chip // 4, lax.rem(chip, 4)
    yh, z = tp // 4, lax.rem(tp, 4)
    rows_own = g32.shape[1]
    n_rows = qraw.shape[0]
    batch = n_rows // STEPS
    half = n_rows // 2

    def chip_at(offset, sign=1):
        hi, lo = shifted(yl, x, offset, sign)
        return hi * 4 + lo

    def tp_at(offset, sign=1):
        hi, lo = shifted(yh, z, offset, sign)
        return hi * 4 + lo

    sibling = (rep + 1 - 2 * core, tp)

    def plane_dev(offset, sign=1):
        return (chip_at(offset, sign) * 2 + core, tp)

    def across(dx):
        return (((1 - yl) * 4 + lax.rem(x + dx, 4)) * 2 + core, (1 - yh) * 4 + z)

    width = hsend.shape[2]
    h_copies = []
    for k in range(8):
        col = pl.multiple_of(chip_at(OFFSETS[k]) * width, 128)
        src = hid_hbm.at[z, :, pl.ds(col, width)]
        dst = hsend.at[k] if k < 7 else hbuf.at[7, z]
        c = pltpu.make_async_copy(src, dst, in_sem.at[k])
        c.start()
        h_copies.append(c)

    g_copies = []
    for own in (0, 1):
        for k in range(8):
            block = chip_at(OFFSETS[k]) * 2 + (core if own else 1 - core)
            c = pltpu.make_async_copy(g_hbm.at[block], g32.at[own * 8 + k], g_sem.at[own * 8 + k])
            c.start()
            g_copies.append(c)
    barrier = pltpu.get_barrier_semaphore()
    pl.semaphore_signal(barrier, inc=1, device_id=sibling, device_id_type=MESH)
    for dx in range(4):
        pl.semaphore_signal(barrier, inc=1, device_id=across(dx), device_id_type=MESH)
    for k in range(7):
        pl.semaphore_signal(barrier, inc=1, device_id=plane_dev(OFFSETS[k]), device_id_type=MESH)
        pl.semaphore_signal(barrier, inc=1, device_id=(rep, tp_at(TP_OFFSETS[k])), device_id_type=MESH)
    sent = []

    def send(src, dst, send_sem, recv_sem, device):
        c = pltpu.make_async_remote_copy(
            src_ref=src, dst_ref=dst, send_sem=send_sem, recv_sem=recv_sem,
            device_id=device, device_id_type=MESH)
        c.start()
        sent.append(c)
        return c

    s0_copies = []

    def share(n):
        s0_copies.append(send(s0.at[n], r0.at[n], s0_send.at[n], s0_recv.at[n], sibling))

    early = 3
    for k in range(early):
        g_copies[k].wait()
        s0[k] = g32[k].astype(BF16)
    pl.semaphore_wait(barrier, 19)
    for k in range(early):
        share(k)

    h1_copies = []
    for k, (dy, dx) in enumerate(OFFSETS):
        h_copies[k].wait()
        if k < 7:
            h1_copies.append(send(
                hsend.at[k], hbuf.at[k, z], h1_send.at[k], h1_recv.at[k],
                across(dx) if dy else plane_dev((0, dx))))
    for k in range(early, 8):
        g_copies[k].wait()
        s0[k] = g32[k].astype(BF16)
        share(k)

    small = [
        pltpu.make_async_copy(q_hbm, qraw, in_sem.at[8]),
        pltpu.make_async_copy(len_hbm, lens, in_sem.at[9]),
        pltpu.make_async_copy(par_hbm, par, in_sem.at[10]),
        pltpu.make_async_copy(mom_hbm, mom, in_sem.at[11]),
    ]
    for c in small:
        c.start()
    kv_copies = []
    for r in range(batch):
        ck = pltpu.make_async_copy(cache_hbm.at[0, r], kbuf.at[r], k_sem.at[r])
        cv = pltpu.make_async_copy(cache_hbm.at[1, r], vbuf.at[r], v_sem.at[r])
        ck.start()
        cv.start()
        kv_copies.append((ck, cv))
    wo_copy = pltpu.make_async_copy(wo_hbm, wo, in_sem.at[12])
    wo_copy.start()

    upper = c1s.shape[1]
    c1_copies, d1_copies = {}, {}
    for k, (dy, dx) in enumerate(OFFSETS):
        s0_copies[k].wait_recv()
        g_copies[8 + k].wait()
        both = g32[8 + k] + r0[k].astype(F32)
        if dy:
            c1s[dx] = both[:upper].astype(BF16)
            c1_copies[dx] = send(
                c1s.at[dx], c1r.at[dx], c1_send.at[dx], c1_recv.at[dx], plane_dev((1, 0)))
        else:
            g32[8 + k, :upper, :] = both[:upper]
        if dx:
            d1s[dx, dy] = both[upper:].astype(BF16)
            if not dy:
                d1_copies[dx] = send(
                    d1s.at[dx], d1r.at[dx], d1_send.at[dx], d1_recv.at[dx], plane_dev((0, dx)))
        else:
            g32[8 + k, upper:, :] = both[upper:]
    slot_of = {offset: 8 + k for k, offset in enumerate(OFFSETS)}

    for c in small:
        c.wait()
    for g in range(GROUP):
        part = qraw[:, g * HD:(g + 1) * HD]
        for h in range(2):
            qb[h, g * half:(g + 1) * half, :] = part[h * half:(h + 1) * half]
        qf[g * n_rows:(g + 1) * n_rows, :] = part.astype(F32)
    qf[GROUP * n_rows:, :] = jnp.zeros((qf.shape[0] - GROUP * n_rows, HD), F32)

    scale = HD ** -0.5
    per_row = qf.shape[0] // batch

    def attend(rows):
        results = []
        for r in rows:
            for c in kv_copies[r]:
                c.wait()
        for r in rows:
            q = qf[pl.ds(r, per_row, stride=batch), :].astype(BF16)
            scores = lax.dot_general(
                q, kbuf[r], (((1,), (1,)), ((), ())), preferred_element_type=F32) * scale
            slot = lax.broadcasted_iota(jnp.int32, scores.shape, 1)
            scores = jnp.where(slot < lens[r], scores, MASKED)
            top = jnp.max(scores, axis=1, keepdims=True)
            weight = jnp.exp(scores - top)
            mass = jnp.sum(weight, axis=1, keepdims=True)
            mixed = jnp.dot(weight.astype(BF16), vbuf[r], preferred_element_type=F32)
            results.append((r, top, mass, mixed))
        for r, top, mass, mixed in results:
            at = pl.ds(r, per_row, stride=batch)
            acc[at, :] = mixed
            peak[at, :] = jnp.broadcast_to(top, mixed.shape)
            total[at, :] = jnp.broadcast_to(mass, mixed.shape)

    attend(range(0, 2))
    c2_copies = []
    for n, dx in enumerate((2, 1, 3)):
        c1_copies[dx].wait_recv()
        c2s[dx] = (g32[slot_of[0, dx], :upper, :] + c1r[dx].astype(F32)).astype(BF16)
        for dx in ((), (1, 2), (3,))[n]:
            c2_copies.append(send(c2s.at[dx], c2r.at[dx], c2_send.at[dx], c2_recv.at[dx], plane_dev((0, dx))))
        if n == 0:
            for c in h1_copies:
                c.wait_recv()
            h2_copies = []
            for m in range(1, 4):
                h2_copies.append(send(
                    hbuf.at[:, z], hbuf.at[:, z], h2_send.at[m], h2_recv.at[m], (rep, tp_at((0, m)))))
        attend(range(2 + 2 * n, 4 + 2 * n))
    lower_sum = g32[slot_of[1, 0], upper:, :]
    for dx in (2, 1, 3):
        d1_copies[dx].wait_recv()
        lower_sum = lower_sum + d1r[dx, 1].astype(F32)
    d2s[...] = lower_sum.astype(BF16)
    d2_copy = send(d2s, d2r, d2_send.at[0], d2_recv.at[0], plane_dev((1, 0)))
    attend(range(8, 12))
    attend(range(14, 16))
    row = lax.broadcasted_iota(jnp.int32, (n_rows, HD), 0)
    lane = lax.broadcasted_iota(jnp.int32, (n_rows, HD), 1)
    position = row // batch
    for r in range(batch):
        position = position + jnp.where(lax.rem(row, batch) == r, lens[r], 0)
    power = lax.rem(lane, HD // 2).astype(F32) * (-2.0 / HD)
    angle = position.astype(F32) * jnp.exp(power * jnp.log(jnp.float32(ROPE_BASE)))
    cos_t[...] = jnp.cos(angle)
    sine = jnp.sin(angle)
    sin_t[...] = jnp.where(lane < HD // 2, -sine, sine)

    def outer_step(rows, summed):
        grad = summed * (1.0 / REPLICAS)
        moved = OUTER_DECAY * mom[rows, :] + grad
        stepped = par[rows, :] - OUTER_RATE * (grad + OUTER_DECAY * moved)
        newm[rows, :] = moved
        newp[rows, :] = stepped
        wbuf[core, rows, :] = stepped.astype(BF16)

    mine = slot_of[0, 0]
    w_copies = []
    d2_copy.wait_recv()
    lower_sum = g32[mine, upper:, :] + d2r[...].astype(F32)
    for dx in (1, 2, 3):
        lower_sum = lower_sum + d1r[dx, 0].astype(F32)
    outer_step(slice(upper, rows_own), lower_sum)
    lower = rows_own - upper
    w_copies.append(send(
        wbuf.at[core, pl.ds(upper, lower)], wbuf.at[core, pl.ds(upper, lower)], w_send.at[1], w_recv.at[1],
        sibling))
    c1_copies[0].wait_recv()
    upper_sum = g32[mine, :upper, :] + c1r[0].astype(F32)
    for n, dx in enumerate((1, 2, 3)):
        c2_copies[n].wait_recv()
        upper_sum = upper_sum + c2r[dx].astype(F32)
    outer_step(slice(0, upper), upper_sum)
    w_copies.append(send(
        wbuf.at[core, pl.ds(0, upper)], wbuf.at[core, pl.ds(0, upper)], w_send.at[0], w_recv.at[0], sibling))
    attend(range(12, 14))

    for c in h2_copies:
        c.wait_recv()
    for c in w_copies:
        c.wait_recv()
    weights = wbuf[...].reshape(2 * rows_own, wbuf.shape[2])
    f_copies, fresh = [], []
    for h in range(2):
        states = hbuf[:, h * (STEPS // 2):(h + 1) * (STEPS // 2)].reshape(8 * half, width)
        part = jnp.dot(states, weights, preferred_element_type=F32)
        at = pl.ds(h * half, half)
        for k in range(7):
            fsend[k, at, :] = part[k * half:(k + 1) * half].astype(BF16)
            f_copies.append(send(
                fsend.at[k, at], frecv.at[k, at], f_send.at[7 * h + k], f_recv.at[7 * h + k],
                plane_dev(OFFSETS[k], -1)))
        fresh.append(part[7 * half:])
    o_copies, owned = [], []
    out_width = lob.shape[1]
    keys, values = [], []
    for h in range(2):
        at = pl.ds(h * half, half)
        now = fresh[h]
        for k in range(7):
            f_copies[7 * h + k].wait_recv()
            now = now + frecv[k, at, :].astype(F32)
        key_part = now[:, :HD]
        turned = pltpu.roll(key_part, HD // 2, 1)
        keys.append((key_part * cos_t[at, :] + turned * sin_t[at, :]).astype(BF16))
        values.append(now[:, HD:].astype(BF16))
        kvb[at, :HD] = keys[h]
        kvb[at, HD:] = values[h]

        def gather(ref):
            return jnp.concatenate(
                [ref[g * n_rows + h * half:g * n_rows + (h + 1) * half, :] for g in range(GROUP)], axis=0)

        scores = lax.dot_general(
            qb[h], jnp.concatenate(keys, axis=0), (((1,), (1,)), ((), ())), preferred_element_type=F32) * scale
        q_row = lax.broadcasted_iota(jnp.int32, scores.shape, 0)
        k_row = lax.broadcasted_iota(jnp.int32, scores.shape, 1)
        q_at = lax.rem(q_row, half) + h * half
        allowed = (lax.rem(q_at, batch) == lax.rem(k_row, batch)) & (k_row <= q_at)
        scores = jnp.where(allowed, scores, MASKED)
        old_top = gather(peak)[:, :1]
        top = jnp.maximum(old_top, jnp.max(scores, axis=1, keepdims=True))
        weight = jnp.exp(scores - top)
        shrink = jnp.exp(old_top - top)
        mass = gather(total)[:, :1] * shrink + jnp.sum(weight, axis=1, keepdims=True)
        mixed = gather(acc) * shrink + jnp.dot(
            weight.astype(BF16), jnp.concatenate(values, axis=0), preferred_element_type=F32)
        mixed = (mixed / mass).astype(BF16)
        attention = jnp.concatenate([mixed[g * half:(g + 1) * half] for g in range(GROUP)], axis=1)

        if h == 0:
            wo_copy.wait()
        for k in range(8):
            col = pl.multiple_of(tp_at(TP_OFFSETS[k]) * out_width, 128)
            part = jnp.dot(attention, wo[:, pl.ds(col, out_width)], preferred_element_type=F32)
            if k < 7:
                osend[k, at, :] = part.astype(BF16)
                o_copies.append(send(
                    osend.at[k, at], orecv.at[k, at], o_send.at[7 * h + k], o_recv.at[7 * h + k],
                    (rep, tp_at(TP_OFFSETS[k]))))
            else:
                owned.append(part)
    for h in range(2):
        at = pl.ds(h * half, half)
        now = owned[h]
        for k in range(7):
            o_copies[7 * h + k].wait_recv()
            now = now + orecv[k, at, :].astype(F32)
        lob[at, :] = now.astype(BF16)
    for c in sent:
        c.wait_send()


def finish(*refs):
    ins, outs, sem = refs[:4], refs[4:8], refs[8]
    copies = [pltpu.make_async_copy(a, b, sem.at[i]) for i, (a, b) in enumerate(zip(ins, outs))]
    for c in copies:
        c.start()
    for c in copies:
        c.wait()


def per_device(
    pseudo_grads, outer_params, momentum, hidden_in, queries, cache, lengths, out_weight
):
    own, columns = outer_params.shape
    steps, batch, model = hidden_in.shape
    n_rows = steps * batch
    slots = cache.shape[2]
    features, out_all = out_weight.shape
    width = 2 * own
    out_width = out_all // 8
    g = pseudo_grads.reshape(REPLICAS, own, columns)
    dma = pltpu.SemaphoreType.DMA
    vm = pltpu.VMEM
    per_row = 24
    upper = 192
    scratch = [
        vm((16, own, columns), F32),
        vm((8, own, columns), BF16),
        vm((8, own, columns), BF16),
        vm((4, upper, columns), BF16),
        vm((4, upper, columns), BF16),
        vm((4, upper, columns), BF16),
        vm((4, upper, columns), BF16),
        vm((4, 2, own - upper, columns), BF16),
        vm((4, 2, own - upper, columns), BF16),
        vm((own - upper, columns), BF16),
        vm((own - upper, columns), BF16),
        vm((own, columns), F32),
        vm((own, columns), F32),
        vm((2, own, columns), BF16),
        vm((8, batch, width), BF16),
        vm((8, steps, batch, width), BF16),
        vm((8, n_rows, columns), BF16),
        vm((8, n_rows, columns), BF16),
        vm((n_rows, features), BF16),
        vm((per_row * batch, HD), F32),
        vm((2, GROUP * n_rows // 2, HD), BF16),
        vm((batch, slots, HD), BF16),
        vm((batch, slots, HD), BF16),
        pltpu.SMEM((batch,), jnp.int32),
        vm((features, out_all), BF16),
        vm((per_row * batch, HD), F32),
        vm((per_row * batch, HD), F32),
        vm((per_row * batch, HD), F32),
        vm((n_rows, HD), F32),
        vm((n_rows, HD), F32),
        vm((8, n_rows, out_width), BF16),
        vm((8, n_rows, out_width), BF16),
        dma((16,)), dma((batch,)), dma((batch,)), dma((13,)),
    ]
    for n in (8, 4, 4, 4, 1, 8, 4, 2, 14, 14):
        scratch += [dma((n,)), dma((n,))]
    any_spec = pl.BlockSpec(memory_space=pl.ANY)
    new_params, new_momentum, new_kv, layer_out = pl.pallas_call(
        kernel,
        out_shape=(
            pltpu.VMEM((own, columns), F32),
            pltpu.VMEM((own, columns), F32),
            pltpu.VMEM((n_rows, columns), BF16),
            pltpu.VMEM((n_rows, out_width), BF16),
        ),
        in_specs=[any_spec] * 8,
        out_specs=(pl.BlockSpec(memory_space=pltpu.VMEM),) * 4,
        scratch_shapes=scratch,
        compiler_params=pltpu.CompilerParams(
            collective_id=0, has_side_effects=True, vmem_limit_bytes=56 * 1024 * 1024),
        name="outer_step_decode",
    )(
        *(pltpu.with_memory_space_constraint(a, pltpu.HBM) for a in (
            g, outer_params, momentum, hidden_in, queries.reshape(n_rows, features),
            cache, lengths, out_weight)),
    )
    new_params, new_momentum, new_kv, layer_out = pl.pallas_call(
        finish,
        out_shape=tuple(jax.ShapeDtypeStruct(a.shape, a.dtype) for a in (new_params, new_momentum, new_kv, layer_out)),
        in_specs=[any_spec] * 4,
        out_specs=(any_spec,) * 4,
        scratch_shapes=[dma((4,))],
        name="finish",
    )(*(pltpu.with_memory_space_constraint(a, pltpu.VMEM) for a in (new_params, new_momentum, new_kv, layer_out)))
    return (
        new_params, new_momentum,
        new_kv.reshape(steps, batch, columns),
        layer_out.reshape(steps, batch, out_width),
    )


def solution(mesh):
    placed = (
        P("rep", None, "tp"),
        P("rep", "tp"),
        P("rep", "tp"),
        P(None, "rep", None),
        P(None, "rep", "tp"),
        P(None, "rep", None, "tp"),
        P("rep"),
        P("tp", None),
    )
    return jax.shard_map(
        per_device,
        mesh=mesh,
        in_specs=placed,
        out_specs=(P("rep", "tp"), P("rep", "tp"), P(None, "rep", "tp"), P(None, "rep", "tp")),
        check_vma=False,
    )
```
